32 devices in a mesh: batch: 8 (over z, core), seq: 4 (over y, x).
Axes of the slice: x: 2, y: 2, z: 4, core: 2. Of those that a mesh axis runs over, the one named last changes fastest.
Arguments:
- tokens: bfloat16 [8, 1024, 2048], P('batch', 'seq'), may hold values from -6 to 6
- segments: int32 [8, 1024], P('batch', 'seq'), may hold values from 0 to 5, as said below
- positions: int32 [8, 1024], P('batch', 'seq'), may hold values from 0 to 1023, as said below
- cotangent: bfloat16 [8, 1024, 2048], P('batch', 'seq'), may hold values from -6 to 6
- ln_gain: bfloat16 [2048], P(('batch', 'seq')), may hold values from 0.099609375 to 1.8984375
- ln_bias: bfloat16 [2048], P(('batch', 'seq')), may hold values from -3 to 3
- in_weight: bfloat16 [2048, 14336], P(('batch', 'seq')), may hold values from -0.125 to 0.125
- in_bias: bfloat16 [14336], P(('batch', 'seq')), may hold values from -3 to 3
- proj_weight: bfloat16 [2048, 2048], P(('batch', 'seq')), may hold values from -0.5 to 0.5
- down_weight: bfloat16 [8192, 2048], P(('batch', 'seq')), may hold values from -0.09375 to 0.09375
- out_bias: bfloat16 [2048], P(('batch', 'seq')), may hold values from -3 to 3
Outputs:
- out: bfloat16 [8, 1024, 2048], P('batch', 'seq')
- grad_tokens: bfloat16 [8, 1024, 2048], P('batch', 'seq')
- grad_ln_gain: float32 [2048], P(('batch', 'seq'))
- grad_ln_bias: float32 [2048], P(('batch', 'seq'))
- grad_in_weight: float32 [2048, 14336], P(('batch', 'seq'))
- grad_in_bias: float32 [14336], P(('batch', 'seq'))
- grad_proj_weight: float32 [2048, 2048], P(('batch', 'seq'))
- grad_down_weight: float32 [8192, 2048], P(('batch', 'seq'))
- grad_out_bias: float32 [2048], P(('batch', 'seq'))
The draws below stay inside these ranges and needn't reach their ends.
Inputs may be any that keep to these rules, and one draw needn't show every extreme that they name: `segments`: within each sequence the document numbers start at 0 and rise by one at each document's first token; every document holds 200 to 2000 tokens except the last, which the sequence's end may cut. `positions`: 0 at a document's first token, rising by one along the document.
All inputs are finite; a program needn't handle non-finite values.
Results may differ from the reference program's by a relative error of at most 0.0095.
Values may be sent and summed in bfloat16 or wider, within the bound.
No kernel may reach another device: no remote copies, remote signals or barrier semaphores. Data moves between devices by JAX's collectives and lax.ppermute only.
A program may use at most 448 MiB of HBM per device.

```python
import jax
import jax.numpy as jnp
from jax import lax

D = 2048
HD = 64
ROT = 32
FF = 8192
DOC_MIN = 200
DOC_MAX = 2000
LENGTH = 1024
SEQS = 8
E = 14336


def document_ends(key):
    count = LENGTH // DOC_MIN + 1
    drawn = jax.random.randint(jax.random.fold_in(key, 11), (SEQS, count), DOC_MIN, DOC_MAX + 1)
    seq_index = jnp.arange(SEQS, dtype=jnp.int32)[:, None]
    doc_index = jnp.arange(count, dtype=jnp.int32)[None, :]
    drawn = jnp.where((seq_index == 0) & (doc_index == 0), DOC_MAX, drawn)
    drawn = jnp.where(seq_index == SEQS - 1, DOC_MIN, drawn)
    return jnp.cumsum(drawn, axis=1).astype(jnp.int32)


def draw_segments(key, part):
    ends = document_ends(key)
    places = jnp.arange(LENGTH, dtype=jnp.int32)
    passed = (ends[:, None, :] <= places[None, :, None]).astype(jnp.int32)
    return jnp.sum(passed, axis=2).astype(jnp.int32)


def draw_positions(key, part):
    ends = document_ends(key)
    places = jnp.arange(LENGTH, dtype=jnp.int32)
    starts = jnp.max(jnp.where(ends[:, None, :] <= places[None, :, None], ends[:, None, :], 0), axis=2)
    return (places[None, :] - starts).astype(jnp.int32)


def spiked(entries, key, source, target, shards_of, factor):
    def block_of(axis_at):
        return (jnp.arange(entries.shape[axis_at]) // (entries.shape[axis_at] // shards_of)).reshape((-1,) + (1,) * (entries.ndim - 1 - axis_at))

    one_side = jax.random.permutation(key, shards_of)[block_of(target)]
    second = (block_of(target) + shards_of // 2) % shards_of
    return jnp.where((block_of(source) == one_side) | (block_of(source) == second), factor * entries, entries)


def block_scale(stream_key, shape, shards, least, top_value):
    factor_of = 1.0
    for position, shards_of in shards:
        steps = jax.random.uniform(jax.random.fold_in(jax.random.fold_in(stream_key, 6), position), (shards_of,), jnp.float32, least / len(shards), top_value / len(shards))
        factor_of = factor_of * jnp.repeat(jnp.exp(steps), shape[position] // shards_of).reshape((-1,) + (1,) * (len(shape) - 1 - position))
    return factor_of


def noise(stream_key, extent, scale, limit, shards=(), held_as=jnp.bfloat16):
    values = scale * jax.random.normal(stream_key, extent, jnp.float32)
    if shards:
        values = values * block_scale(stream_key, extent, shards, -0.22, 0.18)
    return jnp.clip(values, -limit, limit).astype(held_as)


def noise_with(rng, dims, scale, bound, split, heavy, kind=jnp.bfloat16):
    values = scale * jax.random.normal(rng, dims, jnp.float32)
    if split:
        values = values * block_scale(rng, dims, split, -0.22, 0.18)
    return jnp.clip(spiked(values, jax.random.fold_in(rng, 3), *heavy), -bound, bound).astype(kind)


def setup_inputs(seed: int = 0) -> dict:
    seeds = jax.random.split(jax.random.key(seed), 12)
    tokens = noise(seeds[0], (SEQS, LENGTH, D), 1.0, 6.0, ((0, 8), (1, 4)))
    segments = draw_segments(jax.random.fold_in(seeds[11], 71), 0)
    positions = draw_positions(jax.random.fold_in(seeds[11], 71), 0)
    cotangent = noise_with(seeds[3], (SEQS, LENGTH, D), 1.0, 6.0, ((0, 8), (1, 4)), (0, 2, 8, 2.0))
    ln_gain = jnp.clip(1.0 + 0.18 * jax.random.normal(seeds[4], (D,), jnp.float32), 0.099609375, 1.8984375).astype(jnp.bfloat16)
    ln_bias = noise(seeds[5], (D,), 0.3, 3.0, ((0, 32),))
    in_weight = noise(seeds[6], (D, E), D ** -0.5, 0.125, ((0, 32),))
    in_bias = noise(seeds[7], (E,), 0.3, 3.0, ((0, 32),))
    proj_weight = noise(seeds[8], (D, D), (D // 16) ** -0.5, 0.5, ((0, 32),))
    down_weight = noise(seeds[9], (FF, D), (FF // 2) ** -0.5, 0.09375, ((0, 32),))
    out_bias = noise(seeds[10], (D,), 0.3, 3.0, ((0, 32),))
    return dict(tokens=tokens, segments=segments, positions=positions, cotangent=cotangent, ln_gain=ln_gain, ln_bias=ln_bias, in_weight=in_weight, in_bias=in_bias, proj_weight=proj_weight, down_weight=down_weight, out_bias=out_bias)


@jax.custom_vjp
def low(v):
    return lax.optimization_barrier(v.astype(jnp.bfloat16)).astype(jnp.float32)

@jax.custom_vjp
def low_back(v):
    return v

def low_keep(v):
    return (low(v), None)

def low_pass(kept, grad):
    return (grad,)

def back_keep(v):
    return (v, None)

def back_low(kept, grad):
    return (low(grad),)
low.defvjp(low_keep, low_pass)
low_back.defvjp(back_keep, back_low)
HIGHEST = lax.Precision.HIGHEST
NEG_LARGE = -1e+30

def rotary_tables(place, rot_dims):
    freq = 10000.0 ** (-(2.0 * jnp.arange(rot_dims // 2).astype(jnp.float32)) / rot_dims)
    theta = place.astype(jnp.float32)[:, None] * freq[None, :]
    return (jnp.cos(theta), jnp.sin(theta))

def rotate(field, cosine, sine):
    half = cosine.shape[1]
    first = field[:, :, :half]
    second = field[:, :, half:2 * half]
    remain = field[:, :, 2 * half:]
    cos_rows = cosine[:, None, :]
    sin_rows = sine[:, None, :]
    return jnp.concatenate([first * cos_rows - second * sin_rows, second * cos_rows + first * sin_rows, remain], axis=2)

def forward_seq(inputs, seg_row, pos_row, ln_gain, ln_bias, in_weight, in_bias, proj_weight, down_weight, out_bias):
    length = inputs.shape[0]
    width = inputs.shape[1]
    heads = width // HD
    centre = lax.optimization_barrier(jnp.mean(inputs, axis=1, keepdims=True))
    centred = inputs - centre
    spread = lax.optimization_barrier(jnp.mean(centred * centred, axis=1, keepdims=True))
    normal = centred * lax.rsqrt(spread + 1e-05)
    normed = low(normal * ln_gain + ln_bias)
    mixed = low_back(jnp.dot(normed, in_weight, precision=HIGHEST) + in_bias)
    cosine, sine = rotary_tables(pos_row, ROT)
    query = low(rotate(mixed[:, :width].reshape(length, heads, HD), cosine, sine))
    key_all = low(rotate(mixed[:, width:2 * width].reshape(length, heads, HD), cosine, sine))
    value_all = low(mixed[:, 2 * width:3 * width].reshape(length, heads, HD))
    activated = low(jax.nn.gelu(mixed[:, 3 * width:], approximate=True))
    block = min(512, length)
    count = length // block
    places = jnp.arange(length, dtype=jnp.int32)

    def attend(item):
        query_block, seg_block, index_block = item
        raw_scores = jnp.einsum('qhd,khd->hqk', query_block, key_all, precision=HIGHEST) * HD ** (-0.5)
        scores = low_back(raw_scores)
        allowed = (seg_block[:, None] == seg_row[None, :]) & (places[None, :] <= index_block[:, None])
        scores = jnp.where(allowed[None], scores, NEG_LARGE)
        probs = jax.nn.softmax(scores, axis=-1)
        return jnp.einsum('hqk,khd->qhd', low(probs), value_all, precision=HIGHEST)
    attended = lax.map(jax.checkpoint(attend), (query.reshape(count, block, heads, HD), seg_row.reshape(count, block), places.reshape(count, block)))
    attended = low_back(low(attended.reshape(length, width)))
    return inputs + jnp.dot(attended, proj_weight, precision=HIGHEST) + jnp.dot(activated, down_weight, precision=HIGHEST) + out_bias

def reference(tokens, segments, positions, cotangent, ln_gain, ln_bias, in_weight, in_bias, proj_weight, down_weight, out_bias):
    params = tuple((weight_item.astype(jnp.float32) for weight_item in (ln_gain, ln_bias, in_weight, in_bias, proj_weight, down_weight, out_bias)))

    def one_seq(totals, item):
        token_row, seg_row, pos_row, cot_row = item

        def forward(inputs, *weights):
            return forward_seq(inputs, seg_row, pos_row, *weights)
        result, pull = jax.vjp(forward, token_row.astype(jnp.float32), *params)
        grads = pull(cot_row.astype(jnp.float32))
        totals = tuple((total + grad for total, grad in zip(totals, grads[1:])))
        return (totals, (result.astype(jnp.bfloat16), grads[0].astype(jnp.bfloat16)))
    zeros = tuple((jnp.zeros_like(weight_item) for weight_item in params))
    totals, (outputs, grad_tokens) = lax.scan(one_seq, zeros, (tokens, segments, positions, cotangent))
    return (outputs, grad_tokens) + totals
```

```python
import functools

import jax
import jax.numpy as jnp
from jax import lax
from jax.experimental import pallas as pl
from jax.experimental.pallas import tpu as pltpu
from jax.sharding import PartitionSpec as P

HD = 64
ROT = 32
NEG_LARGE = -1e30
NORM_EPS = 1e-05
CORES = 2
f32 = jnp.float32
bf16 = jnp.bfloat16
BOTH = ("batch", "seq")
NN = ((1,), (0,))
NT = ((1,), (1,))
TN = ((0,), (0,))


def dot(left, right, dims):
    return lax.dot_general(left, right, (dims, ((), ())), preferred_element_type=f32)


def swap_halves(x):
    width = x.shape[1]
    lane = lax.broadcasted_iota(jnp.int32, x.shape, 1) % HD
    return jnp.where(
        lane < ROT // 2, pltpu.roll(x, width - ROT // 2, 1), pltpu.roll(x, ROT // 2, 1)
    )


def attention_kernel(
    block, mixed_ref, grad_ref, cos_ref, sin_ref, start_ref, out_ref, dmixed_ref, q_s, k_s, v_s, o_s, dq_s, dk_s, dv_s
):
    head = pl.program_id(1)
    length, width = grad_ref.shape
    scale = HD**-0.5

    def wide(ref):
        table = ref[...]
        return jnp.concatenate([table] * (width // table.shape[1]), axis=1)

    @pl.when(head == 0)
    def _():
        cosine, sine = wide(cos_ref), wide(sin_ref)
        q = mixed_ref[:, 0:width]
        q_s[...] = ((q * cosine + swap_halves(q) * sine).astype(bf16) * scale).astype(bf16)
        k = mixed_ref[:, width : 2 * width]
        k_s[...] = (k * cosine + swap_halves(k) * sine).astype(bf16)
        v_s[...] = mixed_ref[:, 2 * width : 3 * width].astype(bf16)
        o_s[...] = jnp.zeros_like(o_s)
        dq_s[...] = jnp.zeros_like(dq_s)
        dk_s[...] = jnp.zeros_like(dk_s)
        dv_s[...] = jnp.zeros_like(dv_s)

    mine = lax.broadcasted_iota(jnp.int32, (1, width), 1) // HD == head
    zero = jnp.zeros((), bf16)
    for i in range(length // block):
        rows = pl.ds(i * block, block)
        reach = (i + 1) * block
        q = jnp.where(mine, q_s[rows, :], zero)
        grad = jnp.where(mine, grad_ref[rows, :], zero)
        k = k_s[0:reach, :]
        v = v_s[0:reach, :]
        scores = dot(q, k, NT)
        key_at = lax.broadcasted_iota(jnp.int32, (block, reach), 1)
        query_at = i * block + lax.broadcasted_iota(jnp.int32, (block, reach), 0)
        allowed = (key_at <= query_at) & (key_at >= start_ref[rows, :])
        scores = jnp.where(allowed, scores, NEG_LARGE)
        probs = jnp.exp(scores - jnp.max(scores, axis=1, keepdims=True))
        probs = probs * (1.0 / jnp.sum(probs, axis=1, keepdims=True))
        low = probs.astype(bf16)
        o_s[rows, :] = jnp.where(mine, dot(low, v, NN), o_s[rows, :])
        dprobs = dot(grad, v, NT)
        delta = jnp.sum(probs * dprobs, axis=1, keepdims=True)
        dscores = (probs * (dprobs - delta)).astype(bf16)
        dq_s[rows, :] = jnp.where(mine, dot(dscores, k, NN), dq_s[rows, :])
        dk_s[0:reach, :] += dot(dscores, q, TN)
        dv_s[0:reach, :] += dot(low, grad, TN)

    @pl.when(head == pl.num_programs(1) - 1)
    def _():
        cosine, sine = wide(cos_ref), wide(sin_ref)
        out_ref[...] = o_s[...].astype(bf16)
        dq = dq_s[...] * scale
        dmixed_ref[:, 0:width] = (dq * cosine - swap_halves(dq) * sine).astype(bf16)
        dk = dk_s[...]
        dmixed_ref[:, width : 2 * width] = (dk * cosine - swap_halves(dk) * sine).astype(bf16)
        dmixed_ref[:, 2 * width : 3 * width] = dv_s[...].astype(bf16)


def attention(mixed, grad, cosine, sine, start, length):
    tokens, width = grad.shape

    def rows(columns):
        return pl.BlockSpec((length, columns), lambda s, h: (s, 0))

    return pl.pallas_call(
        functools.partial(attention_kernel, min(256, length)),
        grid=(tokens // length, width // HD),
        in_specs=[rows(3 * width), rows(width), rows(cosine.shape[1]), rows(cosine.shape[1]), rows(1)],
        out_specs=[rows(width), rows(3 * width)],
        out_shape=[
            jax.ShapeDtypeStruct((tokens, width), bf16),
            jax.ShapeDtypeStruct((tokens, 3 * width), bf16),
        ],
        scratch_shapes=[pltpu.VMEM((length, width), bf16)] * 3 + [pltpu.VMEM((length, width), f32)] * 4,
        compiler_params=pltpu.CompilerParams(vmem_limit_bytes=48 * 1024 * 1024),
        cost_estimate=pl.CostEstimate(
            flops=40 * tokens * length * width, bytes_accessed=16 * tokens * width, transcendentals=0
        ),
    )(mixed, grad, cosine, sine, start)


def rotary_wide(place, width=128):
    lane = jnp.arange(width) % HD
    freq = 10000.0 ** (-(2.0 * (lane % (ROT // 2)).astype(f32)) / ROT)
    theta = place.astype(f32)[:, None] * freq[None, :]
    cosine = jnp.where(lane < ROT, jnp.cos(theta), 1.0)
    sine = jnp.sin(theta)
    sine = jnp.where(lane < ROT // 2, -sine, jnp.where(lane < ROT, sine, 0.0))
    return cosine, sine


def gelu_parts(u):
    a = (2.0 / jnp.pi) ** 0.5
    t = jnp.tanh(a * (u + 0.044715 * u * u * u))
    value = 0.5 * u * (1.0 + t)
    slope = 0.5 * (1.0 + t) + 0.5 * u * (1.0 - t * t) * a * (1.0 + 3 * 0.044715 * u * u)
    return value, slope


def build(n_batch, n_seq):
    ranks = CORES * n_seq
    planes = n_batch // CORES
    n_dev = n_batch * n_seq
    plane_groups = [[z * ranks + r for r in range(ranks)] for z in range(planes)]
    line_groups = [[z * CORES + c for z in range(planes)] for c in range(CORES)]

    def gather_plane(x):
        return lax.all_gather(x, BOTH, axis_index_groups=plane_groups, axis=0, tiled=True)

    def scatter_plane(x):
        return lax.psum_scatter(
            x, BOTH, axis_index_groups=plane_groups, scatter_dimension=0, tiled=True
        )

    def swap_plane(x):
        return lax.all_to_all(x, BOTH, 0, 0, axis_index_groups=plane_groups, tiled=True)

    def gather_line(x):
        return lax.all_gather(x, "batch", axis_index_groups=line_groups, axis=0, tiled=True)

    def scatter_line(x):
        return lax.psum_scatter(
            x, "batch", axis_index_groups=line_groups, scatter_dimension=0, tiled=True
        )

    def shards(
        tokens, segments, positions, cotangent, ln_gain, ln_bias, in_weight, in_bias, proj_weight, down_weight, out_bias
    ):
        rows, width = tokens.shape[1:]
        length = rows * n_seq
        in_rows, total = in_weight.shape
        proj_rows, down_rows = proj_weight.shape[0], down_weight.shape[0]
        hidden = total - 3 * width
        chunks = 2
        part = down_rows // chunks
        whole_heads = proj_rows % HD == 0
        head_groups = planes if whole_heads else 1
        head_cols = width // (head_groups * ranks)
        mine_cols = width // ranks
        index = lax.axis_index("batch") * n_seq + lax.axis_index("seq")
        rank = index % ranks

        small = jnp.concatenate([in_bias, ln_gain, ln_bias, out_bias])
        small_all = lax.all_to_all(
            jnp.broadcast_to(small[None], (n_dev, small.shape[0])), BOTH, 0, 0, tiled=True
        ).astype(f32)
        n_bias = in_bias.shape[0]
        n_width = ln_gain.shape[0]
        bias_all = small_all[:, :n_bias].reshape(-1)
        gain_all = small_all[:, n_bias : n_bias + n_width].reshape(-1)
        shift_all = small_all[:, n_bias + n_width : n_bias + 2 * n_width].reshape(-1)
        out_bias_all = small_all[:, n_bias + 2 * n_width :].reshape(-1)
        place = lax.all_to_all(
            jnp.broadcast_to(positions, (ranks, rows)), BOTH, 0, 0, axis_index_groups=plane_groups, tiled=True
        ).reshape(-1)

        def split_heads(x):
            lead = x.shape[0]
            x = x.reshape(lead, 3, head_groups, ranks, head_cols)
            return jnp.transpose(x, (3, 0, 1, 2, 4)).reshape(ranks, lead, 3 * mine_cols)

        def split_hidden(x, c):
            lead = x.shape[0]
            x = x.reshape(lead, planes, ranks, chunks, part)[:, :, :, c]
            return jnp.transpose(x, (2, 0, 1, 3)).reshape(ranks, lead, planes * part)

        def join_heads(x):
            lead = x.shape[1]
            x = x.reshape(ranks, lead, 3, head_groups, head_cols)
            return jnp.transpose(x, (1, 2, 3, 0, 4)).reshape(lead, 3 * width)

        def join_hidden(xs):
            lead = xs[0].shape[1]
            x = jnp.stack([x.reshape(ranks, lead, planes, part) for x in xs])
            return jnp.transpose(x, (2, 3, 1, 0, 4)).reshape(lead, hidden)

        bias_heads = lax.dynamic_index_in_dim(
            split_heads(bias_all[None, : 3 * width]), rank, 0, keepdims=False
        )
        bias_hidden = [
            lax.dynamic_index_in_dim(split_hidden(bias_all[None, 3 * width :], c), rank, 0, keepdims=False)
            for c in range(chunks)
        ]

        def in_columns(x):
            return gather_line(swap_plane(x).reshape(ranks * in_rows, x.shape[2]))

        down = [gather_line(down_weight[c * part : (c + 1) * part]) for c in range(chunks)]
        w_hidden = [in_columns(split_hidden(in_weight[:, 3 * width :], c)) for c in range(chunks)]
        w_heads = in_columns(split_heads(in_weight[:, : 3 * width]))
        if whole_heads:
            proj = gather_line(proj_weight)
        else:
            proj = lax.dynamic_slice_in_dim(
                lax.all_gather(proj_weight, BOTH, axis=0, tiled=True), rank * mine_cols, mine_cols, 0
            )

        token_all = gather_plane(tokens[0])
        grad_all = gather_plane(cotangent[0])

        wide = token_all.astype(f32)
        centred = wide - jnp.mean(wide, axis=1, keepdims=True)
        inv_std = lax.rsqrt(jnp.mean(centred * centred, axis=1, keepdims=True) + NORM_EPS)
        normed = (centred * inv_std * gain_all + shift_all).astype(bf16)

        activated, grad_u, grad_down, grad_hidden = [], [], [], []
        for c in range(chunks):
            u = dot(normed, w_hidden[c], NN) + bias_hidden[c]
            value, slope = gelu_parts(u)
            act = value.astype(bf16)
            du = (dot(grad_all, down[c], NT) * slope).astype(bf16)
            activated.append(act)
            grad_u.append(du)
            grad_down.append(scatter_line(dot(act, grad_all, TN).astype(bf16)))
            grad_hidden.append(scatter_line(dot(normed, du, TN).astype(bf16)))

        mixed = dot(normed, w_heads, NN) + bias_heads
        grad_attended = dot(grad_all, proj, NT).astype(bf16)
        cosine, sine = rotary_wide(place)
        start = (jnp.arange(place.shape[0], dtype=jnp.int32) % length - place)[:, None]
        attended, grad_mixed = attention(mixed, grad_attended, cosine, sine, start, length)
        grad_proj = dot(attended, grad_all, TN).astype(bf16)
        if whole_heads:
            grad_proj = scatter_line(grad_proj).astype(f32)
        else:
            grad_proj = lax.psum_scatter(
                lax.dynamic_update_slice_in_dim(
                    jnp.zeros((width, width), f32), grad_proj.astype(f32), rank * mine_cols, 0
                ),
                BOTH, scatter_dimension=0, tiled=True,
            )
        grad_heads = scatter_line(dot(normed, grad_mixed, TN).astype(bf16))

        out = dot(attended, proj, NN)
        for c in range(chunks):
            out = out + dot(activated[c], down[c], NN)
        grad_normed = dot(grad_mixed, w_heads, NT)
        for c in range(chunks):
            grad_normed = grad_normed + dot(grad_u[c], w_hidden[c], NT)
        out = scatter_plane(out.astype(bf16)).astype(f32)
        grad_normed = scatter_plane(grad_normed.astype(bf16)).astype(f32)

        own = tokens[0].astype(f32)
        own_grad = cotangent[0].astype(f32)
        result = own + out + out_bias_all
        centred = own - jnp.mean(own, axis=1, keepdims=True)
        inv_std = lax.rsqrt(jnp.mean(centred * centred, axis=1, keepdims=True) + NORM_EPS)
        normal = centred * inv_std
        scaled = grad_normed * gain_all
        grad_tokens = own_grad + inv_std * (
            scaled
            - jnp.mean(scaled, axis=1, keepdims=True)
            - normal * jnp.mean(scaled * normal, axis=1, keepdims=True)
        )

        def full_columns(heads_part, hidden_parts):
            at = (jnp.arange(ranks) == rank)[:, None, None]
            heads_all = join_heads(jnp.where(at, heads_part[None, None], 0.0))
            hidden_all = join_hidden([jnp.where(at, x[None, None], 0.0) for x in hidden_parts])
            return jnp.concatenate([heads_all, hidden_all], axis=1)

        bias_sum = full_columns(
            jnp.sum(grad_mixed.astype(f32), axis=0), [jnp.sum(x.astype(f32), axis=0) for x in grad_u]
        )
        sums = jnp.concatenate(
            [
                bias_sum.reshape(n_dev, n_bias),
                jnp.sum(grad_normed * normal, axis=0).reshape(n_dev, n_width),
                jnp.sum(grad_normed, axis=0).reshape(n_dev, n_width),
                jnp.sum(own_grad, axis=0).reshape(n_dev, n_width),
            ],
            axis=1,
        )
        sums = jnp.sum(lax.all_to_all(sums, BOTH, 0, 0, tiled=True), axis=0)

        def own_columns(x):
            return swap_plane(x.reshape(ranks, in_rows, x.shape[1]))

        grad_in = jnp.concatenate(
            [join_heads(own_columns(grad_heads)), join_hidden([own_columns(x) for x in grad_hidden])], axis=1
        ).astype(f32)
        return (
            result.astype(bf16)[None],
            grad_tokens.astype(bf16)[None],
            sums[n_bias : n_bias + n_width],
            sums[n_bias + n_width : n_bias + 2 * n_width],
            grad_in,
            sums[:n_bias],
            grad_proj,
            jnp.concatenate(grad_down, axis=0).astype(f32),
            sums[n_bias + 2 * n_width :],
        )

    return shards


def solution(mesh):
    placed = (
        P("batch", "seq", None),
        P("batch", "seq"),
        P("batch", "seq"),
        P("batch", "seq", None),
        P(("batch", "seq")),
        P(("batch", "seq")),
        P(("batch", "seq"), None),
        P(("batch", "seq")),
        P(("batch", "seq"), None),
        P(("batch", "seq"), None),
        P(("batch", "seq")),
    )
    return jax.shard_map(
        build(mesh.shape["batch"], mesh.shape["seq"]),
        mesh=mesh,
        in_specs=placed,
        out_specs=(
            P("batch", "seq", None),
            P("batch", "seq", None),
            P(("batch", "seq")),
            P(("batch", "seq")),
            P(("batch", "seq"), None),
            P(("batch", "seq")),
            P(("batch", "seq"), None),
            P(("batch", "seq"), None),
            P(("batch", "seq")),
        ),
        check_vma=False,
    )
```

```python
import functools

import jax
import jax.numpy as jnp
from jax import lax
from jax.experimental import pallas as pl
from jax.experimental.pallas import tpu as pltpu
from jax.sharding import PartitionSpec as P

HD = 64
ROT = 32
NEG_LARGE = -1e30
NORM_EPS = 1e-05
CORES = 2
f32 = jnp.float32
bf16 = jnp.bfloat16
BOTH = ("batch", "seq")
NN = ((1,), (0,))
NT = ((1,), (1,))
TN = ((0,), (0,))


def dot(left, right, dims):
    return lax.dot_general(left, right, (dims, ((), ())), preferred_element_type=f32)


def swap_halves(x):
    width = x.shape[1]
    lane = lax.broadcasted_iota(jnp.int32, x.shape, 1) % HD
    return jnp.where(
        lane < ROT // 2, pltpu.roll(x, width - ROT // 2, 1), pltpu.roll(x, ROT // 2, 1)
    )


def attention_kernel(
    block, mixed_ref, grad_ref, cos_ref, sin_ref, start_ref, out_ref, dmixed_ref, q_s, k_s, v_s, o_s, dq_s, dk_s, dv_s
):
    head = pl.program_id(1)
    length, width = grad_ref.shape
    scale = HD**-0.5

    def wide(ref):
        table = ref[...]
        return jnp.concatenate([table] * (width // table.shape[1]), axis=1)

    @pl.when(head == 0)
    def _():
        cosine, sine = wide(cos_ref), wide(sin_ref)
        q = mixed_ref[:, 0:width]
        q_s[...] = ((q * cosine + swap_halves(q) * sine).astype(bf16) * scale).astype(bf16)
        k = mixed_ref[:, width : 2 * width]
        k_s[...] = (k * cosine + swap_halves(k) * sine).astype(bf16)
        v_s[...] = mixed_ref[:, 2 * width : 3 * width].astype(bf16)
        o_s[...] = jnp.zeros_like(o_s)
        dq_s[...] = jnp.zeros_like(dq_s)
        dk_s[...] = jnp.zeros_like(dk_s)
        dv_s[...] = jnp.zeros_like(dv_s)

    mine = lax.broadcasted_iota(jnp.int32, (1, width), 1) // HD == head
    zero = jnp.zeros((), bf16)
    for i in range(length // block):
        rows = pl.ds(i * block, block)
        reach = (i + 1) * block
        q = jnp.where(mine, q_s[rows, :], zero)
        grad = jnp.where(mine, grad_ref[rows, :], zero)
        k = k_s[0:reach, :]
        v = v_s[0:reach, :]
        scores = dot(q, k, NT)
        key_at = lax.broadcasted_iota(jnp.int32, (block, reach), 1)
        query_at = i * block + lax.broadcasted_iota(jnp.int32, (block, reach), 0)
        allowed = (key_at <= query_at) & (key_at >= start_ref[rows, :])
        scores = jnp.where(allowed, scores, NEG_LARGE)
        probs = jnp.exp(scores - jnp.max(scores, axis=1, keepdims=True))
        probs = probs * (1.0 / jnp.sum(probs, axis=1, keepdims=True))
        low = probs.astype(bf16)
        o_s[rows, :] = jnp.where(mine, dot(low, v, NN), o_s[rows, :])
        dprobs = dot(grad, v, NT)
        delta = jnp.sum(probs * dprobs, axis=1, keepdims=True)
        dscores = (probs * (dprobs - delta)).astype(bf16)
        dq_s[rows, :] = jnp.where(mine, dot(dscores, k, NN), dq_s[rows, :])
        dk_s[0:reach, :] += dot(dscores, q, TN)
        dv_s[0:reach, :] += dot(low, grad, TN)

    @pl.when(head == pl.num_programs(1) - 1)
    def _():
        cosine, sine = wide(cos_ref), wide(sin_ref)
        out_ref[...] = o_s[...].astype(bf16)
        dq = dq_s[...] * scale
        dmixed_ref[:, 0:width] = (dq * cosine - swap_halves(dq) * sine).astype(bf16)
        dk = dk_s[...]
        dmixed_ref[:, width : 2 * width] = (dk * cosine - swap_halves(dk) * sine).astype(bf16)
        dmixed_ref[:, 2 * width : 3 * width] = dv_s[...].astype(bf16)


def attention(mixed, grad, cosine, sine, start, length):
    tokens, width = grad.shape

    def rows(columns):
        return pl.BlockSpec((length, columns), lambda s, h: (s, 0))

    return pl.pallas_call(
        functools.partial(attention_kernel, min(256, length)),
        grid=(tokens // length, width // HD),
        in_specs=[rows(3 * width), rows(width), rows(cosine.shape[1]), rows(cosine.shape[1]), rows(1)],
        out_specs=[rows(width), rows(3 * width)],
        out_shape=[
            jax.ShapeDtypeStruct((tokens, width), bf16),
            jax.ShapeDtypeStruct((tokens, 3 * width), bf16),
        ],
        scratch_shapes=[pltpu.VMEM((length, width), bf16)] * 3 + [pltpu.VMEM((length, width), f32)] * 4,
        compiler_params=pltpu.CompilerParams(vmem_limit_bytes=48 * 1024 * 1024),
        cost_estimate=pl.CostEstimate(
            flops=40 * tokens * length * width, bytes_accessed=16 * tokens * width, transcendentals=0
        ),
    )(mixed, grad, cosine, sine, start)


def rotary_wide(place, width=128):
    lane = jnp.arange(width) % HD
    freq = 10000.0 ** (-(2.0 * (lane % (ROT // 2)).astype(f32)) / ROT)
    theta = place.astype(f32)[:, None] * freq[None, :]
    cosine = jnp.where(lane < ROT, jnp.cos(theta), 1.0)
    sine = jnp.sin(theta)
    sine = jnp.where(lane < ROT // 2, -sine, jnp.where(lane < ROT, sine, 0.0))
    return cosine, sine


def gelu_parts(u):
    a = (2.0 / jnp.pi) ** 0.5
    t = jnp.tanh(a * (u + 0.044715 * u * u * u))
    value = 0.5 * u * (1.0 + t)
    slope = 0.5 * (1.0 + t) + 0.5 * u * (1.0 - t * t) * a * (1.0 + 3 * 0.044715 * u * u)
    return value, slope


def params():
    return pltpu.CompilerParams(vmem_limit_bytes=48 * 1024 * 1024)


def norm_kernel(steps, own_ref, other_ref, gain_ref, shift_ref, out_ref):
    def write(x):
        x = x.astype(f32)
        centred = x - jnp.mean(x, axis=1, keepdims=True)
        inv_std = lax.rsqrt(jnp.mean(centred * centred, axis=1, keepdims=True) + NORM_EPS)
        out_ref[...] = (centred * inv_std * gain_ref[...] + shift_ref[...]).astype(bf16)

    @pl.when(pl.program_id(0) < steps)
    def _():
        write(own_ref[...])

    @pl.when(pl.program_id(0) >= steps)
    def _():
        write(other_ref[...])


def join_kernel(steps, own_ref, other_ref, out_ref):
    @pl.when(pl.program_id(0) < steps)
    def _():
        out_ref[...] = own_ref[...]

    @pl.when(pl.program_id(0) >= steps)
    def _():
        out_ref[...] = other_ref[...]


def over_both(kernel, own, other, *rest):
    tokens, width = own.shape
    block = min(256, tokens)
    steps = tokens // block
    whole = pl.BlockSpec((1, width), lambda i: (0, 0))
    return pl.pallas_call(
        functools.partial(kernel, steps),
        grid=(2 * steps,),
        in_specs=[
            pl.BlockSpec((block, width), lambda i: (jnp.minimum(i, steps - 1), 0)),
            pl.BlockSpec((block, width), lambda i: (jnp.maximum(i - steps, 0), 0)),
        ]
        + [whole] * len(rest),
        out_specs=pl.BlockSpec((block, width), lambda i: (i, 0)),
        out_shape=jax.ShapeDtypeStruct((2 * tokens, width), bf16),
        compiler_params=params(),
        cost_estimate=pl.CostEstimate(flops=16 * tokens * width, bytes_accessed=8 * tokens * width, transcendentals=0),
    )(own, other, *[x[None] for x in rest])


def hidden_kernel(normed_ref, grad_ref, up_ref, down_ref, bias_ref, act_ref, du_ref, sum_ref):
    u = dot(normed_ref[...], up_ref[...], NN) + bias_ref[...]
    grad = dot(grad_ref[...], down_ref[...], NT)
    value, slope = gelu_parts(u)
    act_ref[...] = value.astype(bf16)
    du = (grad * slope).astype(bf16)
    du_ref[...] = du

    @pl.when(pl.program_id(0) == 0)
    def _():
        sum_ref[...] = jnp.zeros_like(sum_ref)

    sum_ref[...] += jnp.sum(du.astype(f32), axis=0, keepdims=True)


def hidden_layer(normed, grad, up, down, bias):
    tokens, width = normed.shape
    units = up.shape[1]
    block = min(256, tokens)
    rows = pl.BlockSpec((block, width), lambda i: (i, 0))
    part = pl.BlockSpec((block, units), lambda i: (i, 0))

    def whole(shape):
        return pl.BlockSpec(shape, lambda i: (0, 0))

    return pl.pallas_call(
        hidden_kernel,
        grid=(tokens // block,),
        in_specs=[rows, rows, whole((width, units)), whole((units, width)), whole((1, units))],
        out_specs=[part, part, whole((1, units))],
        out_shape=[
            jax.ShapeDtypeStruct((tokens, units), bf16),
            jax.ShapeDtypeStruct((tokens, units), bf16),
            jax.ShapeDtypeStruct((1, units), f32),
        ],
        compiler_params=params(),
        cost_estimate=pl.CostEstimate(
            flops=4 * tokens * width * units, bytes_accessed=4 * tokens * width, transcendentals=0
        ),
    )(normed, grad, up, down, bias[None])


def heads_kernel(normed_ref, grad_ref, in_ref, proj_ref, bias_ref, mixed_ref, dout_ref):
    mixed_ref[...] = dot(normed_ref[...], in_ref[...], NN) + bias_ref[...]
    dout_ref[...] = dot(grad_ref[...], proj_ref[...], NT).astype(bf16)


def heads_layer(normed, grad, weight, proj, bias):
    tokens, width = normed.shape
    columns, inner = weight.shape[1], proj.shape[0]
    block = min(256, tokens)
    rows = pl.BlockSpec((block, width), lambda i: (i, 0))

    def whole(shape):
        return pl.BlockSpec(shape, lambda i: (0, 0))

    return pl.pallas_call(
        heads_kernel,
        grid=(tokens // block,),
        in_specs=[rows, rows, whole((width, columns)), whole((inner, width)), whole((1, columns))],
        out_specs=[pl.BlockSpec((block, columns), lambda i: (i, 0)), pl.BlockSpec((block, inner), lambda i: (i, 0))],
        out_shape=[
            jax.ShapeDtypeStruct((tokens, columns), f32),
            jax.ShapeDtypeStruct((tokens, inner), bf16),
        ],
        compiler_params=params(),
        cost_estimate=pl.CostEstimate(
            flops=2 * tokens * width * (columns + inner), bytes_accessed=4 * tokens * width, transcendentals=0
        ),
    )(normed, grad, weight, proj, bias[None])


def joined_kernel(count, dims, first_ref, *refs):
    total = dot(refs[0][...], refs[count][...], dims)
    for i in range(1, count):
        total += dot(refs[i][...], refs[count + i][...], dims)
    refs[2 * count][...] = total.astype(bf16)


def joined_product(lefts, rights, dims, first, tokens):
    count = len(lefts)
    columns = rights[0].shape[1 if dims is NN else 0]
    block = min(256, tokens)
    steps = tokens // block
    rights_specs = [pl.BlockSpec(x.shape, lambda i, first: (0, 0)) for x in rights]
    return pl.pallas_call(
        functools.partial(joined_kernel, count, dims),
        grid_spec=pltpu.PrefetchScalarGridSpec(
            num_scalar_prefetch=1,
            grid=(steps,),
            in_specs=[pl.BlockSpec((block, x.shape[1]), lambda i, first: (first[0] * steps + i, 0)) for x in lefts]
            + rights_specs,
            out_specs=pl.BlockSpec((block, columns), lambda i, first: (i, 0)),
        ),
        out_shape=jax.ShapeDtypeStruct((tokens, columns), bf16),
        compiler_params=params(),
        cost_estimate=pl.CostEstimate(
            flops=2 * tokens * columns * sum(x.shape[1] for x in lefts), bytes_accessed=4 * tokens * columns,
            transcendentals=0,
        ),
    )(first[None], *lefts, *rights)


def after(x, *others):
    if not others:
        return x
    return lax.optimization_barrier((x,) + others)[0]


def build(n_batch, n_seq):
    ranks = CORES * n_seq
    planes = n_batch // CORES
    n_dev = n_batch * n_seq
    plane_groups = [[z * ranks + r for r in range(ranks)] for z in range(planes)]
    line_groups = [[z * CORES + c for z in range(planes)] for c in range(CORES)]

    def seq_permute(x, bit):
        return lax.ppermute(x, "seq", [(s, s ^ bit) for s in range(n_seq)])

    def core_permute(x):
        return lax.ppermute(x, "batch", [(b, b ^ 1) for b in range(n_batch)])

    def take(x, i):
        return lax.dynamic_index_in_dim(x, i, 0, keepdims=False)

    def two(flag, mine, theirs, axis):
        return jnp.where(flag == 0, jnp.stack([mine, theirs], axis), jnp.stack([theirs, mine], axis))

    def gather_plane(x, core, seq):
        if n_seq != 4:
            whole = lax.all_gather(x, BOTH, axis_index_groups=plane_groups, axis=0, tiled=True)
            whole = whole.reshape((CORES, n_seq * x.shape[0]) + x.shape[1:])
            return take(whole, core), take(whole, 1 - core), whole
        bit_x, bit_y = seq % 2, seq // 2
        half = x.shape[1] // 2
        left, right = x[:, :half], x[:, half:]
        left = two(bit_y, left, seq_permute(left, 2), 0)
        right = two(bit_x, right, seq_permute(right, 1), 0)
        early = left
        left = two(bit_x, left, seq_permute(left, 1), 1)
        right = two(bit_y, right, seq_permute(right, 2), 0)
        own = jnp.concatenate([left, right], axis=3).reshape(4 * x.shape[0], x.shape[1])
        return own, core_permute(own), early

    def scatter_plane(product, tokens, core, seq):
        if n_seq != 4:
            both = [product(core ^ i) for i in range(CORES)]
            return lax.psum_scatter(
                jnp.concatenate(both), BOTH, axis_index_groups=plane_groups, scatter_dimension=0, tiled=True
            ).astype(f32)
        other = core_permute(product(jnp.int32(1)))
        x = product(jnp.int32(0)).astype(f32) + other.astype(f32)
        x = x.astype(bf16).reshape(2, 2, tokens // n_seq, x.shape[1])
        bit_x, bit_y = seq % 2, seq // 2
        half = x.shape[3] // 2
        left, right = x[..., :half], x[..., half:]
        by_x = jnp.swapaxes(left, 0, 1)
        from_x = seq_permute(take(by_x, 1 - bit_x), 1)
        from_y = seq_permute(take(right, 1 - bit_y), 2)
        left = (take(by_x, bit_x).astype(f32) + from_x.astype(f32)).astype(bf16)
        right = (take(right, bit_y).astype(f32) + from_y.astype(f32)).astype(bf16)
        from_y = seq_permute(take(left, 1 - bit_y), 2)
        from_x = seq_permute(take(right, 1 - bit_x), 1)
        left = take(left, bit_y).astype(f32) + from_y.astype(f32)
        right = take(right, bit_x).astype(f32) + from_x.astype(f32)
        return jnp.concatenate([left, right], axis=1)

    def swap_plane(x):
        return lax.all_to_all(x, BOTH, 0, 0, axis_index_groups=plane_groups, tiled=True)

    def gather_line(x):
        return lax.all_gather(x, "batch", axis_index_groups=line_groups, axis=0, tiled=True)

    def scatter_line(x):
        return lax.psum_scatter(
            x, "batch", axis_index_groups=line_groups, scatter_dimension=0, tiled=True
        )

    class Chain:
        def __init__(self, x, plane):
            self.x, self.plane, self.step = x, plane, 0
            self.up = self.down = None

        def hop(self, *others):
            self.step += 1
            left = planes - self.step
            up = take(self.x, jnp.minimum(left + self.plane, planes - 1))
            down = take(self.x, jnp.maximum(self.plane - left, 0))
            if self.step > 1:
                up = (up.astype(f32) + self.up.astype(f32)).astype(bf16)
                down = (down.astype(f32) + self.down.astype(f32)).astype(bf16)
            up, down = after(up, *others), after(down, *others)
            self.up = lax.ppermute(up, "batch", [(b, b + CORES) for b in range(CORES * self.step)])
            self.down = lax.ppermute(down, "batch", [(b, b - CORES) for b in range(CORES * left, n_batch)])
            return self.up, self.down

        def result(self):
            while self.step < planes - 1:
                self.hop()
            return take(self.x, self.plane).astype(f32) + self.up.astype(f32) + self.down.astype(f32)

    def shards(
        tokens, segments, positions, cotangent, ln_gain, ln_bias, in_weight, in_bias, proj_weight, down_weight, out_bias
    ):
        rows, width = tokens.shape[1:]
        length = rows * n_seq
        in_rows, total = in_weight.shape
        proj_rows, down_rows = proj_weight.shape[0], down_weight.shape[0]
        hidden = total - 3 * width
        chunks = 2
        part = down_rows // chunks
        whole_heads = proj_rows % HD == 0
        head_groups = planes if whole_heads else 1
        head_cols = width // (head_groups * ranks)
        mine_cols = width // ranks
        index = lax.axis_index("batch") * n_seq + lax.axis_index("seq")
        rank = index % ranks
        plane = index // ranks
        core, seq = rank // n_seq, rank % n_seq

        def split_heads(x):
            lead = x.shape[0]
            x = x.reshape(lead, 3, head_groups, ranks, head_cols)
            return jnp.transpose(x, (3, 0, 1, 2, 4)).reshape(ranks, lead, 3 * mine_cols)

        def split_hidden(x, c):
            lead = x.shape[0]
            x = x.reshape(lead, planes, ranks, chunks, part)[:, :, :, c]
            return jnp.transpose(x, (2, 0, 1, 3)).reshape(ranks, lead, planes * part)

        def join_heads(x):
            lead = x.shape[1]
            x = x.reshape(ranks, lead, 3, head_groups, head_cols)
            return jnp.transpose(x, (1, 2, 3, 0, 4)).reshape(lead, 3 * width)

        def join_hidden(xs):
            lead = xs[0].shape[1]
            x = jnp.stack([x.reshape(ranks, lead, planes, part) for x in xs])
            return jnp.transpose(x, (2, 3, 1, 0, 4)).reshape(lead, hidden)

        def swap_columns(x):
            return swap_plane(x).reshape(ranks * in_rows, x.shape[2])

        hidden_send = [swap_columns(split_hidden(in_weight[:, 3 * width :], 0))]
        later = [split_heads(in_weight[:, : 3 * width])]
        later += [split_hidden(in_weight[:, 3 * width :], c) for c in range(1, chunks)]
        later = swap_columns(after(jnp.concatenate(later, axis=2), hidden_send[0]))
        heads_send = later[:, : 3 * mine_cols]
        for c in range(1, chunks):
            at = 3 * mine_cols + (c - 1) * planes * part
            hidden_send.append(later[:, at : at + planes * part])
        token_halves = gather_plane(tokens[0], core, seq)
        grad_halves = gather_plane(after(cotangent[0], token_halves[2]), core, seq)
        small = jnp.concatenate([x.astype(f32) for x in (in_bias, ln_gain, ln_bias, out_bias, positions[0])])
        small_all = lax.all_to_all(
            jnp.broadcast_to(after(small, token_halves[2])[None], (n_dev, small.shape[0])), BOTH, 0, 0, tiled=True
        )
        n_bias = in_bias.shape[0]
        n_width = ln_gain.shape[0]
        bias_all = small_all[:, :n_bias].reshape(-1)
        gain_all = small_all[:, n_bias : n_bias + n_width].reshape(-1)
        shift_all = small_all[:, n_bias + n_width : n_bias + 2 * n_width].reshape(-1)
        out_bias_all = small_all[:, n_bias + 2 * n_width : n_bias + 3 * n_width].reshape(-1)
        place = small_all[:, n_bias + 3 * n_width :].reshape(planes, CORES, length)
        place = lax.dynamic_index_in_dim(place, plane, 0, keepdims=False).astype(jnp.int32)
        place = jnp.concatenate([take(place, core), take(place, 1 - core)])

        bias_heads = lax.dynamic_index_in_dim(
            split_heads(bias_all[None, : 3 * width]), rank, 0, keepdims=False
        )
        bias_hidden = [
            lax.dynamic_index_in_dim(split_hidden(bias_all[None, 3 * width :], c), rank, 0, keepdims=False)
            for c in range(chunks)
        ]

        def own_columns(x):
            return swap_plane(x.reshape(ranks, in_rows, x.shape[1]))

        own_parts = []
        def pack(main, extra):
            lead, few = extra.shape[:2]
            columns = few * width // main.shape[1]
            extra = extra.reshape(lead, few, width // columns, columns)
            return jnp.concatenate([main, jnp.swapaxes(extra, 1, 2).reshape(lead, -1, columns)], axis=2)

        def unpack(x, few):
            lead, packed, total = x.shape
            columns = few * width // packed
            extra = x[:, :, total - columns :].reshape(lead, width // columns, few, columns)
            return x[:, :, : total - columns], jnp.swapaxes(extra, 1, 2).reshape(lead, few, width)

        down, w_hidden = [None] * chunks, [None] * chunks
        activated, grad_u, sum_u, grad_down, grad_hidden = [], [], [], [], []

        def hidden_part(c, *others):
            act, du, total = hidden_layer(normed, after(grad_all, *others), w_hidden[c], down[c], bias_hidden[c][0])
            activated.append(act)
            grad_u.append(du)
            sum_u.append(total)
            return dot(normed, du, TN).astype(bf16), dot(act, grad_all, TN).astype(bf16)

        normed = over_both(norm_kernel, *token_halves[:2], gain_all, shift_all)
        grad_all = over_both(join_kernel, *grad_halves[:2])
        def gather_hidden(c, *others):
            x = pack(hidden_send[c][None], down_weight[None, c * part : (c + 1) * part])[0]
            x = gather_line(after(x, *others)).reshape(planes, ranks * in_rows, -1)
            x, y = unpack(x, part)
            w_hidden[c], down[c] = x.reshape(width, -1), y.reshape(-1, width)
            return w_hidden[c]

        if whole_heads:
            proj = gather_line(proj_weight)
        else:
            proj = lax.dynamic_slice_in_dim(
                lax.all_gather(proj_weight, BOTH, axis=0, tiled=True), rank * mine_cols, mine_cols, 0
            )
        gather_hidden(0, proj)
        w_heads = gather_line(after(heads_send, proj))
        by_plane = (planes, width // planes, -1)

        def scatter_packed(main, extra, few):
            x = pack(main.reshape(by_plane), extra.reshape(planes, few, width))
            x, y = unpack(scatter_line(x.reshape(width, -1))[None], few)
            return x[0], y[0].astype(f32)

        to_hidden, to_down = hidden_part(0)
        for c in range(1, chunks):
            gather_hidden(c, w_hidden[0], activated[0])
        first, second = scatter_packed(to_hidden, to_down, part)
        grad_hidden.append(first)
        grad_down.append(second)
        hop = ()
        mixed, grad_attended = heads_layer(normed, after(grad_all, to_hidden, to_down, *hidden_send), w_heads, proj, bias_heads[0])
        cosine, sine = rotary_wide(place)
        start = (jnp.arange(place.shape[0], dtype=jnp.int32) % length - place)[:, None]
        attended, grad_mixed = [], []
        for i in range(CORES):
            rows_of = slice(i * length, (i + 1) * length)
            a, m = attention(
                mixed[rows_of], after(grad_attended[rows_of], *hop), cosine[rows_of], sine[rows_of], start[rows_of], length
            )
            attended.append(a)
            grad_mixed.append(m)
        attended, grad_mixed = jnp.concatenate(attended), jnp.concatenate(grad_mixed)
        to_proj = dot(attended, after(grad_all, *hop), TN).astype(bf16)
        to_heads = dot(normed, grad_mixed, TN).astype(bf16)
        if whole_heads:
            grad_heads, grad_proj = scatter_packed(to_heads, to_proj, proj_rows)
        else:
            grad_heads = scatter_line(to_heads)
            grad_proj = lax.psum_scatter(
                lax.dynamic_update_slice_in_dim(
                    jnp.zeros((width, width), f32), to_proj.astype(f32), rank * mine_cols, 0
                ),
                BOTH, scatter_dimension=0, tiled=True,
            )

        last = []
        for c in range(1, chunks):
            to_hidden, to_down = hidden_part(c, to_heads, to_proj)
            last += [to_hidden, to_down]
            grad_hidden.append(scatter_line(to_hidden))
            grad_down.append(scatter_line(to_down).astype(f32))
        bias_heads_sum = jnp.sum(grad_mixed.astype(f32), axis=0)
        attended, grad_mixed = after(attended, *last), after(grad_mixed, *last)
        out = scatter_plane(
            lambda i: joined_product([attended] + activated, [proj] + down, NN, i, length), length, core, seq
        )
        grad_normed = scatter_plane(
            lambda i: joined_product([grad_mixed] + grad_u, [w_heads] + w_hidden, NT, i, length), length, core, seq
        )

        grad_normed = after(grad_normed, grad_proj, grad_heads)
        own = tokens[0].astype(f32)
        own_grad = cotangent[0].astype(f32)
        result = own + out + out_bias_all
        centred = own - jnp.mean(own, axis=1, keepdims=True)
        inv_std = lax.rsqrt(jnp.mean(centred * centred, axis=1, keepdims=True) + NORM_EPS)
        normal = centred * inv_std
        scaled = grad_normed * gain_all
        grad_tokens = own_grad + inv_std * (
            scaled
            - jnp.mean(scaled, axis=1, keepdims=True)
            - normal * jnp.mean(scaled * normal, axis=1, keepdims=True)
        )

        last = [result, grad_tokens]
        grad_hidden[1:] = [after(x, *last) for x in grad_hidden[1:]]
        grad_down[1:] = [after(x, *last) for x in grad_down[1:]]

        def full_columns(heads_part, hidden_parts):
            at = (jnp.arange(ranks) == rank)[:, None, None]
            heads_all = join_heads(jnp.where(at, heads_part[None, None], 0.0))
            hidden_all = join_hidden([jnp.where(at, x[None, None], 0.0) for x in hidden_parts])
            return jnp.concatenate([heads_all, hidden_all], axis=1)

        bias_sum = full_columns(
            bias_heads_sum, [x[0] for x in sum_u]
        )
        sums = jnp.concatenate(
            [
                bias_sum.reshape(n_dev, n_bias),
                jnp.sum(grad_normed * normal, axis=0).reshape(n_dev, n_width),
                jnp.sum(grad_normed, axis=0).reshape(n_dev, n_width),
                jnp.sum(own_grad, axis=0).reshape(n_dev, n_width),
            ],
            axis=1,
        )
        sums = jnp.sum(lax.all_to_all(sums, BOTH, 0, 0, tiled=True), axis=0)

        grad_in = jnp.concatenate(
            [join_heads(own_columns(grad_heads)), join_hidden([own_columns(x) for x in grad_hidden])], axis=1
        ).astype(f32)
        return (
            result.astype(bf16)[None],
            grad_tokens.astype(bf16)[None],
            sums[n_bias : n_bias + n_width],
            sums[n_bias + n_width : n_bias + 2 * n_width],
            grad_in,
            sums[:n_bias],
            grad_proj,
            jnp.concatenate(grad_down, axis=0).astype(f32),
            sums[n_bias + 2 * n_width :],
        )

    return shards


def solution(mesh):
    placed = (
        P("batch", "seq", None),
        P("batch", "seq"),
        P("batch", "seq"),
        P("batch", "seq", None),
        P(("batch", "seq")),
        P(("batch", "seq")),
        P(("batch", "seq"), None),
        P(("batch", "seq")),
        P(("batch", "seq"), None),
        P(("batch", "seq"), None),
        P(("batch", "seq")),
    )
    return jax.shard_map(
        build(mesh.shape["batch"], mesh.shape["seq"]),
        mesh=mesh,
        in_specs=placed,
        out_specs=(
            P("batch", "seq", None),
            P("batch", "seq", None),
            P(("batch", "seq")),
            P(("batch", "seq")),
            P(("batch", "seq"), None),
            P(("batch", "seq")),
            P(("batch", "seq"), None),
            P(("batch", "seq"), None),
            P(("batch", "seq")),
        ),
        check_vma=False,
    )
```

```python
import functools

import jax
import jax.numpy as jnp
from jax import lax
from jax.experimental import pallas as pl
from jax.experimental.pallas import tpu as pltpu
from jax.sharding import PartitionSpec as P

HD = 64
ROT = 32
NEG_LARGE = -1e30
NORM_EPS = 1e-05
CORES = 2
f32 = jnp.float32
bf16 = jnp.bfloat16
BOTH = ("batch", "seq")
NN = ((1,), (0,))
NT = ((1,), (1,))
TN = ((0,), (0,))


def dot(left, right, dims):
    return lax.dot_general(left, right, (dims, ((), ())), preferred_element_type=f32)


def swap_halves(x):
    width = x.shape[1]
    lane = lax.broadcasted_iota(jnp.int32, x.shape, 1) % HD
    return jnp.where(
        lane < ROT // 2, pltpu.roll(x, width - ROT // 2, 1), pltpu.roll(x, ROT // 2, 1)
    )


def attention_kernel(
    block, mixed_ref, grad_ref, cos_ref, sin_ref, start_ref, out_ref, dmixed_ref, q_s, k_s, v_s, o_s, dq_s, dk_s, dv_s
):
    head = pl.program_id(1)
    length, width = grad_ref.shape
    scale = HD**-0.5

    def wide(ref):
        table = ref[...]
        return jnp.concatenate([table] * (width // table.shape[1]), axis=1)

    @pl.when(head == 0)
    def _():
        cosine, sine = wide(cos_ref), wide(sin_ref)
        q = mixed_ref[:, 0:width]
        q_s[...] = ((q * cosine + swap_halves(q) * sine).astype(bf16) * scale).astype(bf16)
        k = mixed_ref[:, width : 2 * width]
        k_s[...] = (k * cosine + swap_halves(k) * sine).astype(bf16)
        v_s[...] = mixed_ref[:, 2 * width : 3 * width].astype(bf16)
        o_s[...] = jnp.zeros_like(o_s)
        dq_s[...] = jnp.zeros_like(dq_s)
        dk_s[...] = jnp.zeros_like(dk_s)
        dv_s[...] = jnp.zeros_like(dv_s)

    mine = lax.broadcasted_iota(jnp.int32, (1, width), 1) // HD == head
    zero = jnp.zeros((), bf16)
    for i in range(length // block):
        rows = pl.ds(i * block, block)
        reach = (i + 1) * block
        q = jnp.where(mine, q_s[rows, :], zero)
        grad = jnp.where(mine, grad_ref[rows, :], zero)
        k = k_s[0:reach, :]
        v = v_s[0:reach, :]
        scores = dot(q, k, NT)
        key_at = lax.broadcasted_iota(jnp.int32, (block, reach), 1)
        query_at = i * block + lax.broadcasted_iota(jnp.int32, (block, reach), 0)
        allowed = (key_at <= query_at) & (key_at >= start_ref[rows, :])
        scores = jnp.where(allowed, scores, NEG_LARGE)
        probs = jnp.exp(scores - jnp.max(scores, axis=1, keepdims=True))
        probs = probs * (1.0 / jnp.sum(probs, axis=1, keepdims=True))
        low = probs.astype(bf16)
        o_s[rows, :] = jnp.where(mine, dot(low, v, NN), o_s[rows, :])
        dprobs = dot(grad, v, NT)
        delta = jnp.sum(probs * dprobs, axis=1, keepdims=True)
        dscores = (probs * (dprobs - delta)).astype(bf16)
        dq_s[rows, :] = jnp.where(mine, dot(dscores, k, NN), dq_s[rows, :])
        dk_s[0:reach, :] += dot(dscores, q, TN)
        dv_s[0:reach, :] += dot(low, grad, TN)

    @pl.when(head == pl.num_programs(1) - 1)
    def _():
        cosine, sine = wide(cos_ref), wide(sin_ref)
        out_ref[...] = o_s[...].astype(bf16)
        dq = dq_s[...] * scale
        dmixed_ref[:, 0:width] = (dq * cosine - swap_halves(dq) * sine).astype(bf16)
        dk = dk_s[...]
        dmixed_ref[:, width : 2 * width] = (dk * cosine - swap_halves(dk) * sine).astype(bf16)
        dmixed_ref[:, 2 * width : 3 * width] = dv_s[...].astype(bf16)


def attention(mixed, grad, cosine, sine, start, length):
    tokens, width = grad.shape

    def rows(columns):
        return pl.BlockSpec((length, columns), lambda s, h: (s, 0))

    return pl.pallas_call(
        functools.partial(attention_kernel, min(256, length)),
        grid=(tokens // length, width // HD),
        in_specs=[rows(3 * width), rows(width), rows(cosine.shape[1]), rows(cosine.shape[1]), rows(1)],
        out_specs=[rows(width), rows(3 * width)],
        out_shape=[
            jax.ShapeDtypeStruct((tokens, width), bf16),
            jax.ShapeDtypeStruct((tokens, 3 * width), bf16),
        ],
        scratch_shapes=[pltpu.VMEM((length, width), bf16)] * 3 + [pltpu.VMEM((length, width), f32)] * 4,
        compiler_params=pltpu.CompilerParams(vmem_limit_bytes=48 * 1024 * 1024),
        cost_estimate=pl.CostEstimate(
            flops=40 * tokens * length * width, bytes_accessed=16 * tokens * width, transcendentals=0
        ),
    )(mixed, grad, cosine, sine, start)


def rotary_wide(place, width=128):
    lane = jnp.arange(width) % HD
    freq = 10000.0 ** (-(2.0 * (lane % (ROT // 2)).astype(f32)) / ROT)
    theta = place.astype(f32)[:, None] * freq[None, :]
    cosine = jnp.where(lane < ROT, jnp.cos(theta), 1.0)
    sine = jnp.sin(theta)
    sine = jnp.where(lane < ROT // 2, -sine, jnp.where(lane < ROT, sine, 0.0))
    return cosine, sine


def gelu_parts(u):
    a = (2.0 / jnp.pi) ** 0.5
    t = jnp.tanh(a * (u + 0.044715 * u * u * u))
    value = 0.5 * u * (1.0 + t)
    slope = 0.5 * (1.0 + t) + 0.5 * u * (1.0 - t * t) * a * (1.0 + 3 * 0.044715 * u * u)
    return value, slope


def params():
    return pltpu.CompilerParams(vmem_limit_bytes=48 * 1024 * 1024)


def norm_kernel(steps, own_ref, other_ref, gain_ref, shift_ref, out_ref):
    def write(x):
        x = x.astype(f32)
        centred = x - jnp.mean(x, axis=1, keepdims=True)
        inv_std = lax.rsqrt(jnp.mean(centred * centred, axis=1, keepdims=True) + NORM_EPS)
        out_ref[...] = (centred * inv_std * gain_ref[...] + shift_ref[...]).astype(bf16)

    @pl.when(pl.program_id(0) < steps)
    def _():
        write(own_ref[...])

    @pl.when(pl.program_id(0) >= steps)
    def _():
        write(other_ref[...])


def join_kernel(steps, own_ref, other_ref, out_ref):
    @pl.when(pl.program_id(0) < steps)
    def _():
        out_ref[...] = own_ref[...]

    @pl.when(pl.program_id(0) >= steps)
    def _():
        out_ref[...] = other_ref[...]


def over_both(kernel, own, other, *rest):
    tokens, width = own.shape
    block = min(256, tokens)
    steps = tokens // block
    whole = pl.BlockSpec((1, width), lambda i: (0, 0))
    return pl.pallas_call(
        functools.partial(kernel, steps),
        grid=(2 * steps,),
        in_specs=[
            pl.BlockSpec((block, width), lambda i: (jnp.minimum(i, steps - 1), 0)),
            pl.BlockSpec((block, width), lambda i: (jnp.maximum(i - steps, 0), 0)),
        ]
        + [whole] * len(rest),
        out_specs=pl.BlockSpec((block, width), lambda i: (i, 0)),
        out_shape=jax.ShapeDtypeStruct((2 * tokens, width), bf16),
        compiler_params=params(),
        cost_estimate=pl.CostEstimate(flops=16 * tokens * width, bytes_accessed=8 * tokens * width, transcendentals=0),
    )(own, other, *[x[None] for x in rest])


def hidden_kernel(normed_ref, grad_ref, up_ref, down_ref, bias_ref, act_ref, du_ref, sum_ref):
    u = dot(normed_ref[...], up_ref[...], NN) + bias_ref[...]
    grad = dot(grad_ref[...], down_ref[...], NT)
    value, slope = gelu_parts(u)
    act_ref[...] = value.astype(bf16)
    du = (grad * slope).astype(bf16)
    du_ref[...] = du

    @pl.when(pl.program_id(0) == 0)
    def _():
        sum_ref[...] = jnp.zeros_like(sum_ref)

    sum_ref[...] += jnp.sum(du.astype(f32), axis=0, keepdims=True)


def hidden_layer(normed, grad, up, down, bias):
    tokens, width = normed.shape
    units = up.shape[1]
    block = min(512, tokens)
    rows = pl.BlockSpec((block, width), lambda i: (i, 0))
    part = pl.BlockSpec((block, units), lambda i: (i, 0))

    def whole(shape):
        return pl.BlockSpec(shape, lambda i: (0, 0))

    return pl.pallas_call(
        hidden_kernel,
        grid=(tokens // block,),
        in_specs=[rows, rows, whole((width, units)), whole((units, width)), whole((1, units))],
        out_specs=[part, part, whole((1, units))],
        out_shape=[
            jax.ShapeDtypeStruct((tokens, units), bf16),
            jax.ShapeDtypeStruct((tokens, units), bf16),
            jax.ShapeDtypeStruct((1, units), f32),
        ],
        compiler_params=params(),
        cost_estimate=pl.CostEstimate(
            flops=4 * tokens * width * units, bytes_accessed=4 * tokens * width, transcendentals=0
        ),
    )(normed, grad, up, down, bias[None])


def heads_kernel(normed_ref, grad_ref, in_ref, proj_ref, bias_ref, mixed_ref, dout_ref):
    mixed_ref[...] = dot(normed_ref[...], in_ref[...], NN) + bias_ref[...]
    dout_ref[...] = dot(grad_ref[...], proj_ref[...], NT).astype(bf16)


def heads_layer(normed, grad, weight, proj, bias):
    tokens, width = normed.shape
    columns, inner = weight.shape[1], proj.shape[0]
    block = min(512, tokens)
    rows = pl.BlockSpec((block, width), lambda i: (i, 0))

    def whole(shape):
        return pl.BlockSpec(shape, lambda i: (0, 0))

    return pl.pallas_call(
        heads_kernel,
        grid=(tokens // block,),
        in_specs=[rows, rows, whole((width, columns)), whole((inner, width)), whole((1, columns))],
        out_specs=[pl.BlockSpec((block, columns), lambda i: (i, 0)), pl.BlockSpec((block, inner), lambda i: (i, 0))],
        out_shape=[
            jax.ShapeDtypeStruct((tokens, columns), f32),
            jax.ShapeDtypeStruct((tokens, inner), bf16),
        ],
        compiler_params=params(),
        cost_estimate=pl.CostEstimate(
            flops=2 * tokens * width * (columns + inner), bytes_accessed=4 * tokens * width, transcendentals=0
        ),
    )(normed, grad, weight, proj, bias[None])


def joined_kernel(count, dims, first_ref, *refs):
    total = dot(refs[0][...], refs[count][...], dims)
    for i in range(1, count):
        total += dot(refs[i][...], refs[count + i][...], dims)
    refs[2 * count][...] = total.astype(bf16)


def joined_product(lefts, rights, dims, first, tokens):
    count = len(lefts)
    columns = rights[0].shape[1 if dims is NN else 0]
    block = min(512, tokens)
    steps = tokens // block
    rights_specs = [pl.BlockSpec(x.shape, lambda i, first: (0, 0)) for x in rights]
    return pl.pallas_call(
        functools.partial(joined_kernel, count, dims),
        grid_spec=pltpu.PrefetchScalarGridSpec(
            num_scalar_prefetch=1,
            grid=(steps,),
            in_specs=[pl.BlockSpec((block, x.shape[1]), lambda i, first: (first[0] * steps + i, 0)) for x in lefts]
            + rights_specs,
            out_specs=pl.BlockSpec((block, columns), lambda i, first: (i, 0)),
        ),
        out_shape=jax.ShapeDtypeStruct((tokens, columns), bf16),
        compiler_params=params(),
        cost_estimate=pl.CostEstimate(
            flops=2 * tokens * columns * sum(x.shape[1] for x in lefts), bytes_accessed=4 * tokens * columns,
            transcendentals=0,
        ),
    )(first[None], *lefts, *rights)


def pack_kernel(main_ref, extra_ref, out_ref):
    main, few = main_ref.shape[2], extra_ref.shape[1]
    columns = out_ref.shape[2] - main
    out_ref[0, :, :main] = main_ref[0]
    for i in range(extra_ref.shape[2] // columns):
        out_ref[0, i * few : (i + 1) * few, main:] = extra_ref[0, :, i * columns : (i + 1) * columns]


def pack(main, extra):
    lead, rows, columns = main.shape
    total = columns + extra.shape[1] * extra.shape[2] // rows

    def block(x):
        return pl.BlockSpec((1,) + x[1:], lambda i: (i, 0, 0))

    return pl.pallas_call(
        pack_kernel,
        grid=(lead,),
        in_specs=[block(main.shape), block(extra.shape)],
        out_specs=block((lead, rows, total)),
        out_shape=jax.ShapeDtypeStruct((lead, rows, total), bf16),
        compiler_params=params(),
        cost_estimate=pl.CostEstimate(flops=0, bytes_accessed=4 * lead * rows * total, transcendentals=0),
    )(main, extra)


def after(x, *others):
    if not others:
        return x
    return lax.optimization_barrier((x,) + others)[0]


def build(n_batch, n_seq):
    ranks = CORES * n_seq
    planes = n_batch // CORES
    n_dev = n_batch * n_seq
    plane_groups = [[z * ranks + r for r in range(ranks)] for z in range(planes)]
    line_groups = [[z * CORES + c for z in range(planes)] for c in range(CORES)]

    def seq_permute(x, bit):
        return lax.ppermute(x, "seq", [(s, s ^ bit) for s in range(n_seq)])

    def core_permute(x):
        return lax.ppermute(x, "batch", [(b, b ^ 1) for b in range(n_batch)])

    def take(x, i):
        return lax.dynamic_index_in_dim(x, i, 0, keepdims=False)

    def two(flag, mine, theirs, axis):
        return jnp.where(flag == 0, jnp.stack([mine, theirs], axis), jnp.stack([theirs, mine], axis))

    def gather_plane(x, core, seq, *others):
        if n_seq != 4:
            whole = lax.all_gather(x, BOTH, axis_index_groups=plane_groups, axis=0, tiled=True)
            whole = whole.reshape((CORES, n_seq * x.shape[0]) + x.shape[1:])
            return take(whole, core), take(whole, 1 - core), whole
        bit_x, bit_y = seq % 2, seq // 2
        half = x.shape[1] // 2
        left, right = x[:, :half], x[:, half:]
        left = two(bit_y, left, seq_permute(left, 2), 0)
        right = two(bit_x, right, seq_permute(right, 1), 0)
        early = left
        left = after(left, *others)
        left = two(bit_x, left, seq_permute(left, 1), 1)
        right = two(bit_y, right, seq_permute(right, 2), 0)
        own = jnp.concatenate([left, right], axis=3).reshape(4 * x.shape[0], x.shape[1])
        return own, core_permute(own), early

    def scatter_plane(product, tokens, core, seq):
        if n_seq != 4:
            both = [product(core ^ i) for i in range(CORES)]
            x = lax.psum_scatter(
                jnp.concatenate(both), BOTH, axis_index_groups=plane_groups, scatter_dimension=0, tiled=True
            ).astype(f32)
            return x, (x, x, x)
        other = core_permute(product(jnp.int32(1)))
        x = product(jnp.int32(0)).astype(f32) + other.astype(f32)
        x = x.astype(bf16).reshape(2, 2, tokens // n_seq, x.shape[1])
        bit_x, bit_y = seq % 2, seq // 2
        half = x.shape[3] // 2
        left, right = x[..., :half], x[..., half:]
        by_x = jnp.swapaxes(left, 0, 1)
        from_x = seq_permute(take(by_x, 1 - bit_x), 1)
        from_y = seq_permute(take(right, 1 - bit_y), 2)
        left = (take(by_x, bit_x).astype(f32) + from_x.astype(f32)).astype(bf16)
        right = (take(right, bit_y).astype(f32) + from_y.astype(f32)).astype(bf16)
        from_y = seq_permute(take(left, 1 - bit_y), 2)
        from_x = seq_permute(take(right, 1 - bit_x), 1)
        stages = (x, left, right)
        left = take(left, bit_y).astype(f32) + from_y.astype(f32)
        right = take(right, bit_x).astype(f32) + from_x.astype(f32)
        return jnp.concatenate([left, right], axis=1), stages

    def swap_plane(x):
        return lax.all_to_all(x, BOTH, 0, 0, axis_index_groups=plane_groups, tiled=True)

    def gather_line(x):
        return lax.all_gather(x, "batch", axis_index_groups=line_groups, axis=0, tiled=True)

    def scatter_line(x):
        return lax.psum_scatter(
            x, "batch", axis_index_groups=line_groups, scatter_dimension=0, tiled=True
        )

    class Chain:
        def __init__(self, x, plane):
            self.x, self.plane, self.step = x, plane, 0
            self.up = self.down = None

        def hop(self, *others):
            self.step += 1
            left = planes - self.step
            up = take(self.x, jnp.minimum(left + self.plane, planes - 1))
            down = take(self.x, jnp.maximum(self.plane - left, 0))
            if self.step > 1:
                up = (up.astype(f32) + self.up.astype(f32)).astype(bf16)
                down = (down.astype(f32) + self.down.astype(f32)).astype(bf16)
            up, down = after(up, *others), after(down, *others)
            self.up = lax.ppermute(up, "batch", [(b, b + CORES) for b in range(CORES * self.step)])
            self.down = lax.ppermute(down, "batch", [(b, b - CORES) for b in range(CORES * left, n_batch)])
            return self.up, self.down

        def result(self):
            while self.step < planes - 1:
                self.hop()
            return take(self.x, self.plane).astype(f32) + self.up.astype(f32) + self.down.astype(f32)

    def shards(
        tokens, segments, positions, cotangent, ln_gain, ln_bias, in_weight, in_bias, proj_weight, down_weight, out_bias
    ):
        rows, width = tokens.shape[1:]
        length = rows * n_seq
        in_rows, total = in_weight.shape
        proj_rows, down_rows = proj_weight.shape[0], down_weight.shape[0]
        hidden = total - 3 * width
        chunks = 2
        part = down_rows // chunks
        whole_heads = proj_rows % HD == 0
        head_groups = planes if whole_heads else 1
        head_cols = width // (head_groups * ranks)
        mine_cols = width // ranks
        index = lax.axis_index("batch") * n_seq + lax.axis_index("seq")
        rank = index % ranks
        plane = index // ranks
        core, seq = rank // n_seq, rank % n_seq

        def split_heads(x):
            lead = x.shape[0]
            x = x.reshape(lead, 3, head_groups, ranks, head_cols)
            return jnp.transpose(x, (3, 0, 1, 2, 4)).reshape(ranks, lead, 3 * mine_cols)

        def split_hidden(x, c):
            lead = x.shape[0]
            x = x.reshape(lead, planes, ranks, chunks, part)[:, :, :, c]
            return jnp.transpose(x, (2, 0, 1, 3)).reshape(ranks, lead, planes * part)

        def join_heads(x):
            lead = x.shape[1]
            x = x.reshape(ranks, lead, 3, head_groups, head_cols)
            return jnp.transpose(x, (1, 2, 3, 0, 4)).reshape(lead, 3 * width)

        def join_hidden(xs):
            lead = xs[0].shape[1]
            x = jnp.stack([x.reshape(ranks, lead, planes, part) for x in xs])
            return jnp.transpose(x, (2, 3, 1, 0, 4)).reshape(lead, hidden)

        def swap_columns(x):
            return swap_plane(x).reshape(ranks * in_rows, x.shape[2])

        units = planes * part
        first_send = swap_columns(
            jnp.concatenate(
                [split_hidden(in_weight[:, 3 * width :], 0), split_heads(in_weight[:, : 3 * width])], axis=2
            )
        )
        token_halves = gather_plane(tokens[0], core, seq)
        grad_halves = gather_plane(after(cotangent[0], token_halves[2]), core, seq)
        small = jnp.concatenate([x.astype(f32) for x in (in_bias, ln_gain, ln_bias, out_bias, positions[0])])
        small_all = lax.all_to_all(
            jnp.broadcast_to(after(small, token_halves[2])[None], (n_dev, small.shape[0])), BOTH, 0, 0, tiled=True
        )
        n_bias = in_bias.shape[0]
        n_width = ln_gain.shape[0]
        bias_all = small_all[:, :n_bias].reshape(-1)
        gain_all = small_all[:, n_bias : n_bias + n_width].reshape(-1)
        shift_all = small_all[:, n_bias + n_width : n_bias + 2 * n_width].reshape(-1)
        out_bias_all = small_all[:, n_bias + 2 * n_width : n_bias + 3 * n_width].reshape(-1)
        place = small_all[:, n_bias + 3 * n_width :].reshape(planes, CORES, length)
        place = lax.dynamic_index_in_dim(place, plane, 0, keepdims=False).astype(jnp.int32)
        place = jnp.concatenate([take(place, core), take(place, 1 - core)])

        bias_heads = lax.dynamic_index_in_dim(
            split_heads(bias_all[None, : 3 * width]), rank, 0, keepdims=False
        )
        bias_hidden = [
            lax.dynamic_index_in_dim(split_hidden(bias_all[None, 3 * width :], c), rank, 0, keepdims=False)
            for c in range(chunks)
        ]

        def own_columns(x):
            return swap_plane(x.reshape(ranks, in_rows, x.shape[1]))

        own_parts = []
        def unpack(x, few):
            lead, packed, total = x.shape
            columns = few * width // packed
            extra = x[:, :, total - columns :].reshape(lead, width // columns, few, columns)
            return x[:, :, : total - columns], jnp.swapaxes(extra, 1, 2).reshape(lead, few, width)

        down, w_hidden = [None] * chunks, [None] * chunks
        activated, grad_u, sum_u, grad_down, grad_hidden = [], [], [], [], []

        def hidden_part(c, *others):
            act, du, total = hidden_layer(normed, after(grad_all, *others), w_hidden[c], down[c], bias_hidden[c][0])
            activated.append(act)
            grad_u.append(du)
            sum_u.append(total)
            return dot(normed, du, TN).astype(bf16), dot(act, grad_all, TN).astype(bf16)

        normed = over_both(norm_kernel, *token_halves[:2], gain_all, shift_all)
        grad_all = over_both(join_kernel, *grad_halves[:2])
        def gather_packed(main, c, *others):
            x = pack(main[None], down_weight[None, c * part : (c + 1) * part])[0]
            x = gather_line(after(x, *others))
            down[c] = unpack(x.reshape(planes, ranks * in_rows, -1), part)[1].reshape(-1, width)
            return x

        if whole_heads:
            proj = gather_line(proj_weight)
        else:
            proj = lax.dynamic_slice_in_dim(
                lax.all_gather(proj_weight, BOTH, axis=0, tiled=True), rank * mine_cols, mine_cols, 0
            )
        x = gather_packed(first_send, 0, proj)
        w_hidden[0], w_heads = x[:, :units], x[:, units : units + 3 * mine_cols]
        for c in range(1, chunks):
            more = split_hidden(in_weight[:, 3 * width :], c)
            w_hidden[c] = gather_packed(swap_columns(after(more, token_halves[0])), c, x, normed, grad_all)[:, :units]
        by_plane = (planes, width // planes, -1)

        def scatter_packed(main, extra, few):
            x = pack(main.reshape(by_plane), extra.reshape(planes, few, width))
            x, y = unpack(scatter_line(x.reshape(width, -1))[None], few)
            return x[0], y[0].astype(f32)

        to_hidden, to_down = hidden_part(0)
        first, second = scatter_packed(to_hidden, to_down, part)
        grad_hidden.append(own_columns(first))
        grad_down.append(second)
        mixed, grad_attended = heads_layer(normed, after(grad_all, to_hidden, to_down), w_heads, proj, bias_heads[0])
        cosine, sine = rotary_wide(place)
        start = (jnp.arange(place.shape[0], dtype=jnp.int32) % length - place)[:, None]
        attended, grad_mixed = attention(mixed, grad_attended, cosine, sine, start, length)
        to_proj = dot(attended, grad_all, TN).astype(bf16)
        to_heads = dot(normed, grad_mixed, TN).astype(bf16)
        if whole_heads:
            grad_heads, grad_proj = scatter_packed(to_heads, to_proj, proj_rows)
        else:
            grad_heads = scatter_line(to_heads)
            grad_proj = lax.psum_scatter(
                lax.dynamic_update_slice_in_dim(
                    jnp.zeros((width, width), f32), to_proj.astype(f32), rank * mine_cols, 0
                ),
                BOTH, scatter_dimension=0, tiled=True,
            )

        last = []
        for c in range(1, chunks):
            last += hidden_part(c, to_heads, to_proj)
        bias_heads_sum = jnp.sum(grad_mixed.astype(f32), axis=0)
        grad_mixed = after(grad_mixed, *last)
        grad_normed, stages = scatter_plane(
            lambda i: joined_product([grad_mixed] + grad_u, [w_heads] + w_hidden, NT, i, length), length, core, seq
        )
        attended = after(attended, *last, stages[0], grad_hidden[0])
        out, more = scatter_plane(
            lambda i: joined_product([attended] + activated, [proj] + down, NN, i, length), length, core, seq
        )
        for c in range(1, chunks):
            to_hidden, to_down = last[2 * c - 2 : 2 * c]
            grad_hidden.append(scatter_line(after(to_hidden, stages[0])))
            grad_down.append(scatter_line(after(to_down, *stages, grad_hidden[c])).astype(f32))

        own = tokens[0].astype(f32)
        own_grad = cotangent[0].astype(f32)
        result = own + out + out_bias_all
        centred = own - jnp.mean(own, axis=1, keepdims=True)
        inv_std = lax.rsqrt(jnp.mean(centred * centred, axis=1, keepdims=True) + NORM_EPS)
        normal = centred * inv_std
        scaled = grad_normed * gain_all
        grad_tokens = own_grad + inv_std * (
            scaled
            - jnp.mean(scaled, axis=1, keepdims=True)
            - normal * jnp.mean(scaled * normal, axis=1, keepdims=True)
        )

        last = [result, grad_tokens]
        grad_hidden[1:] = [after(x, *last) for x in grad_hidden[1:]]
        grad_down[1:] = [after(x, *last) for x in grad_down[1:]]

        def full_columns(heads_part, hidden_parts):
            at = (jnp.arange(ranks) == rank)[:, None, None]
            heads_all = join_heads(jnp.where(at, heads_part[None, None], 0.0))
            hidden_all = join_hidden([jnp.where(at, x[None, None], 0.0) for x in hidden_parts])
            return jnp.concatenate([heads_all, hidden_all], axis=1)

        bias_sum = full_columns(
            bias_heads_sum, [x[0] for x in sum_u]
        )
        sums = jnp.concatenate(
            [
                bias_sum.reshape(n_dev, n_bias),
                jnp.sum(grad_normed * normal, axis=0).reshape(n_dev, n_width),
                jnp.sum(grad_normed, axis=0).reshape(n_dev, n_width),
                jnp.sum(own_grad, axis=0).reshape(n_dev, n_width),
            ],
            axis=1,
        )
        sums = jnp.sum(lax.all_to_all(sums, BOTH, 0, 0, tiled=True), axis=0)

        grad_in = jnp.concatenate(
            [join_heads(own_columns(grad_heads)), join_hidden(grad_hidden[:1] + [own_columns(x) for x in grad_hidden[1:]])], axis=1
        ).astype(f32)
        return (
            result.astype(bf16)[None],
            grad_tokens.astype(bf16)[None],
            sums[n_bias : n_bias + n_width],
            sums[n_bias + n_width : n_bias + 2 * n_width],
            grad_in,
            sums[:n_bias],
            grad_proj,
            jnp.concatenate(grad_down, axis=0).astype(f32),
            sums[n_bias + 2 * n_width :],
        )

    return shards


def solution(mesh):
    placed = (
        P("batch", "seq", None),
        P("batch", "seq"),
        P("batch", "seq"),
        P("batch", "seq", None),
        P(("batch", "seq")),
        P(("batch", "seq")),
        P(("batch", "seq"), None),
        P(("batch", "seq")),
        P(("batch", "seq"), None),
        P(("batch", "seq"), None),
        P(("batch", "seq")),
    )
    return jax.shard_map(
        build(mesh.shape["batch"], mesh.shape["seq"]),
        mesh=mesh,
        in_specs=placed,
        out_specs=(
            P("batch", "seq", None),
            P("batch", "seq", None),
            P(("batch", "seq")),
            P(("batch", "seq")),
            P(("batch", "seq"), None),
            P(("batch", "seq")),
            P(("batch", "seq"), None),
            P(("batch", "seq"), None),
            P(("batch", "seq")),
        ),
        check_vma=False,
    )
```

```python
import functools

import jax
import jax.numpy as jnp
from jax import lax
from jax.experimental import pallas as pl
from jax.experimental.pallas import tpu as pltpu
from jax.sharding import PartitionSpec as P

HD = 64
ROT = 32
NEG_LARGE = -1e30
NORM_EPS = 1e-05
CORES = 2
f32 = jnp.float32
bf16 = jnp.bfloat16
BOTH = ("batch", "seq")
NN = ((1,), (0,))
NT = ((1,), (1,))
TN = ((0,), (0,))


def dot(left, right, dims):
    return lax.dot_general(left, right, (dims, ((), ())), preferred_element_type=f32)


def swap_halves(x):
    width = x.shape[1]
    lane = lax.broadcasted_iota(jnp.int32, x.shape, 1) % HD
    return jnp.where(
        lane < ROT // 2, pltpu.roll(x, width - ROT // 2, 1), pltpu.roll(x, ROT // 2, 1)
    )


def attention_kernel(
    block, mixed_ref, grad_ref, cos_ref, sin_ref, start_ref, out_ref, dmixed_ref, q_s, k_s, v_s, o_s, dq_s, dk_s, dv_s
):
    length, width = grad_ref.shape
    heads = width // HD
    scale = HD**-0.5

    def wide(ref):
        table = ref[...]
        return jnp.concatenate([table] * (width // table.shape[1]), axis=1)

    cosine, sine = wide(cos_ref), wide(sin_ref)
    q = mixed_ref[:, 0:width]
    q_s[...] = ((q * cosine + swap_halves(q) * sine).astype(bf16) * scale).astype(bf16)
    k = mixed_ref[:, width : 2 * width]
    k_s[...] = (k * cosine + swap_halves(k) * sine).astype(bf16)
    v_s[...] = mixed_ref[:, 2 * width : 3 * width].astype(bf16)
    dk_s[...] = jnp.zeros_like(dk_s)
    dv_s[...] = jnp.zeros_like(dv_s)
    lane_head = lax.broadcasted_iota(jnp.int32, (1, width), 1) // HD
    zero = jnp.zeros((), bf16)

    def stack(x):
        return jnp.concatenate([jnp.where(lane_head == h, x, zero) for h in range(heads)])

    def unstack(x):
        total = jnp.where(lane_head == 0, x[:block], 0.0)
        for h in range(1, heads):
            total = jnp.where(lane_head == h, x[h * block : (h + 1) * block], total)
        return total

    for i in range(length // block):
        rows = pl.ds(i * block, block)
        reach = (i + 1) * block
        q = stack(q_s[rows, :])
        grad = stack(grad_ref[rows, :])
        k = k_s[0:reach, :]
        v = v_s[0:reach, :]
        scores = dot(q, k, NT)
        key_at = lax.broadcasted_iota(jnp.int32, (block, reach), 1)
        query_at = i * block + lax.broadcasted_iota(jnp.int32, (block, reach), 0)
        allowed = (key_at <= query_at) & (key_at >= start_ref[rows, :])
        shift = jnp.where(allowed, 0.0, NEG_LARGE)
        scores = (scores.reshape(heads, block, reach) + shift[None]).reshape(heads * block, reach)
        probs = jnp.exp(scores - jnp.max(scores, axis=1, keepdims=True))
        probs = probs * (1.0 / jnp.sum(probs, axis=1, keepdims=True))
        low = probs.astype(bf16)
        o_s[rows, :] = unstack(dot(low, v, NN))
        dprobs = dot(grad, v, NT)
        delta = jnp.sum(probs * dprobs, axis=1, keepdims=True)
        dscores = (probs * (dprobs - delta)).astype(bf16)
        dq_s[rows, :] = unstack(dot(dscores, k, NN))
        dk_s[0:reach, :] += dot(dscores, q, TN)
        dv_s[0:reach, :] += dot(low, grad, TN)

    out_ref[...] = o_s[...].astype(bf16)
    dq = dq_s[...] * scale
    dmixed_ref[:, 0:width] = (dq * cosine - swap_halves(dq) * sine).astype(bf16)
    dk = dk_s[...]
    dmixed_ref[:, width : 2 * width] = (dk * cosine - swap_halves(dk) * sine).astype(bf16)
    dmixed_ref[:, 2 * width : 3 * width] = dv_s[...].astype(bf16)


def attention(mixed, grad, cosine, sine, start, length):
    tokens, width = grad.shape

    def rows(columns):
        return pl.BlockSpec((length, columns), lambda s: (s, 0))

    return pl.pallas_call(
        functools.partial(attention_kernel, min(256, length)),
        grid=(tokens // length,),
        in_specs=[rows(3 * width), rows(width), rows(cosine.shape[1]), rows(cosine.shape[1]), rows(1)],
        out_specs=[rows(width), rows(3 * width)],
        out_shape=[
            jax.ShapeDtypeStruct((tokens, width), bf16),
            jax.ShapeDtypeStruct((tokens, 3 * width), bf16),
        ],
        scratch_shapes=[pltpu.VMEM((length, width), bf16)] * 3 + [pltpu.VMEM((length, width), f32)] * 4,
        compiler_params=pltpu.CompilerParams(vmem_limit_bytes=56 * 1024 * 1024),
        cost_estimate=pl.CostEstimate(
            flops=40 * tokens * length * width, bytes_accessed=16 * tokens * width, transcendentals=0
        ),
    )(mixed, grad, cosine, sine, start)


def rotary_wide(place, width=128):
    lane = jnp.arange(width) % HD
    freq = 10000.0 ** (-(2.0 * (lane % (ROT // 2)).astype(f32)) / ROT)
    theta = place.astype(f32)[:, None] * freq[None, :]
    cosine = jnp.where(lane < ROT, jnp.cos(theta), 1.0)
    sine = jnp.sin(theta)
    sine = jnp.where(lane < ROT // 2, -sine, jnp.where(lane < ROT, sine, 0.0))
    return cosine, sine


def gelu_parts(u):
    a = (2.0 / jnp.pi) ** 0.5
    t = jnp.tanh(a * (u + 0.044715 * u * u * u))
    value = 0.5 * u * (1.0 + t)
    slope = 0.5 * (1.0 + t) + 0.5 * u * (1.0 - t * t) * a * (1.0 + 3 * 0.044715 * u * u)
    return value, slope


def params():
    return pltpu.CompilerParams(vmem_limit_bytes=48 * 1024 * 1024)


def norm_kernel(steps, own_ref, other_ref, gain_ref, shift_ref, out_ref):
    def write(x):
        x = x.astype(f32)
        centred = x - jnp.mean(x, axis=1, keepdims=True)
        inv_std = lax.rsqrt(jnp.mean(centred * centred, axis=1, keepdims=True) + NORM_EPS)
        out_ref[...] = (centred * inv_std * gain_ref[...] + shift_ref[...]).astype(bf16)

    @pl.when(pl.program_id(0) < steps)
    def _():
        write(own_ref[...])

    @pl.when(pl.program_id(0) >= steps)
    def _():
        write(other_ref[...])


def join_kernel(steps, own_ref, other_ref, out_ref):
    @pl.when(pl.program_id(0) < steps)
    def _():
        out_ref[...] = own_ref[...]

    @pl.when(pl.program_id(0) >= steps)
    def _():
        out_ref[...] = other_ref[...]


def over_both(kernel, own, other, *rest):
    tokens, width = own.shape
    block = min(256, tokens)
    steps = tokens // block
    whole = pl.BlockSpec((1, width), lambda i: (0, 0))
    return pl.pallas_call(
        functools.partial(kernel, steps),
        grid=(2 * steps,),
        in_specs=[
            pl.BlockSpec((block, width), lambda i: (jnp.minimum(i, steps - 1), 0)),
            pl.BlockSpec((block, width), lambda i: (jnp.maximum(i - steps, 0), 0)),
        ]
        + [whole] * len(rest),
        out_specs=pl.BlockSpec((block, width), lambda i: (i, 0)),
        out_shape=jax.ShapeDtypeStruct((2 * tokens, width), bf16),
        compiler_params=params(),
        cost_estimate=pl.CostEstimate(flops=16 * tokens * width, bytes_accessed=8 * tokens * width, transcendentals=0),
    )(own, other, *[x[None] for x in rest])


def hidden_kernel(normed_ref, grad_ref, up_ref, down_ref, bias_ref, act_ref, du_ref, sum_ref):
    u = dot(normed_ref[...], up_ref[...], NN) + bias_ref[...]
    grad = dot(grad_ref[...], down_ref[...], NT)
    value, slope = gelu_parts(u)
    act_ref[...] = value.astype(bf16)
    du = (grad * slope).astype(bf16)
    du_ref[...] = du

    @pl.when(pl.program_id(0) == 0)
    def _():
        sum_ref[...] = jnp.zeros_like(sum_ref)

    sum_ref[...] += jnp.sum(du.astype(f32), axis=0, keepdims=True)


def hidden_layer(normed, grad, up, down, bias):
    tokens, width = normed.shape
    units = up.shape[1]
    block = min(512, tokens)
    rows = pl.BlockSpec((block, width), lambda i: (i, 0))
    part = pl.BlockSpec((block, units), lambda i: (i, 0))

    def whole(shape):
        return pl.BlockSpec(shape, lambda i: (0, 0))

    return pl.pallas_call(
        hidden_kernel,
        grid=(tokens // block,),
        in_specs=[rows, rows, whole((width, units)), whole((units, width)), whole((1, units))],
        out_specs=[part, part, whole((1, units))],
        out_shape=[
            jax.ShapeDtypeStruct((tokens, units), bf16),
            jax.ShapeDtypeStruct((tokens, units), bf16),
            jax.ShapeDtypeStruct((1, units), f32),
        ],
        compiler_params=params(),
        cost_estimate=pl.CostEstimate(
            flops=4 * tokens * width * units, bytes_accessed=4 * tokens * width, transcendentals=0
        ),
    )(normed, grad, up, down, bias[None])


def heads_kernel(normed_ref, grad_ref, in_ref, proj_ref, bias_ref, mixed_ref, dout_ref):
    mixed_ref[...] = dot(normed_ref[...], in_ref[...], NN) + bias_ref[...]
    dout_ref[...] = dot(grad_ref[...], proj_ref[...], NT).astype(bf16)


def heads_layer(normed, grad, weight, proj, bias):
    tokens, width = normed.shape
    columns, inner = weight.shape[1], proj.shape[0]
    block = min(512, tokens)
    rows = pl.BlockSpec((block, width), lambda i: (i, 0))

    def whole(shape):
        return pl.BlockSpec(shape, lambda i: (0, 0))

    return pl.pallas_call(
        heads_kernel,
        grid=(tokens // block,),
        in_specs=[rows, rows, whole((width, columns)), whole((inner, width)), whole((1, columns))],
        out_specs=[pl.BlockSpec((block, columns), lambda i: (i, 0)), pl.BlockSpec((block, inner), lambda i: (i, 0))],
        out_shape=[
            jax.ShapeDtypeStruct((tokens, columns), f32),
            jax.ShapeDtypeStruct((tokens, inner), bf16),
        ],
        compiler_params=params(),
        cost_estimate=pl.CostEstimate(
            flops=2 * tokens * width * (columns + inner), bytes_accessed=4 * tokens * width, transcendentals=0
        ),
    )(normed, grad, weight, proj, bias[None])


def joined_kernel(count, dims, first_ref, *refs):
    total = dot(refs[0][...], refs[count][...], dims)
    for i in range(1, count):
        total += dot(refs[i][...], refs[count + i][...], dims)
    refs[2 * count][...] = total.astype(bf16)


def joined_product(lefts, rights, dims, first, tokens):
    count = len(lefts)
    columns = rights[0].shape[1 if dims is NN else 0]
    block = min(512, tokens)
    steps = tokens // block
    rights_specs = [pl.BlockSpec(x.shape, lambda i, first: (0, 0)) for x in rights]
    return pl.pallas_call(
        functools.partial(joined_kernel, count, dims),
        grid_spec=pltpu.PrefetchScalarGridSpec(
            num_scalar_prefetch=1,
            grid=(steps,),
            in_specs=[pl.BlockSpec((block, x.shape[1]), lambda i, first: (first[0] * steps + i, 0)) for x in lefts]
            + rights_specs,
            out_specs=pl.BlockSpec((block, columns), lambda i, first: (i, 0)),
        ),
        out_shape=jax.ShapeDtypeStruct((tokens, columns), bf16),
        compiler_params=params(),
        cost_estimate=pl.CostEstimate(
            flops=2 * tokens * columns * sum(x.shape[1] for x in lefts), bytes_accessed=4 * tokens * columns,
            transcendentals=0,
        ),
    )(first[None], *lefts, *rights)


def pack_kernel(main_ref, extra_ref, out_ref):
    main, few = main_ref.shape[2], extra_ref.shape[1]
    columns = out_ref.shape[2] - main
    out_ref[0, :, :main] = main_ref[0]
    for i in range(extra_ref.shape[2] // columns):
        out_ref[0, i * few : (i + 1) * few, main:] = extra_ref[0, :, i * columns : (i + 1) * columns]


def pack(main, extra):
    lead, rows, columns = main.shape
    total = columns + extra.shape[1] * extra.shape[2] // rows

    def block(x):
        return pl.BlockSpec((1,) + x[1:], lambda i: (i, 0, 0))

    return pl.pallas_call(
        pack_kernel,
        grid=(lead,),
        in_specs=[block(main.shape), block(extra.shape)],
        out_specs=block((lead, rows, total)),
        out_shape=jax.ShapeDtypeStruct((lead, rows, total), bf16),
        compiler_params=params(),
        cost_estimate=pl.CostEstimate(flops=0, bytes_accessed=4 * lead * rows * total, transcendentals=0),
    )(main, extra)


def after(x, *others):
    if not others:
        return x
    return lax.optimization_barrier((x,) + others)[0]


def build(n_batch, n_seq):
    ranks = CORES * n_seq
    planes = n_batch // CORES
    n_dev = n_batch * n_seq
    plane_groups = [[z * ranks + r for r in range(ranks)] for z in range(planes)]
    line_groups = [[z * CORES + c for z in range(planes)] for c in range(CORES)]

    def seq_permute(x, bit):
        return lax.ppermute(x, "seq", [(s, s ^ bit) for s in range(n_seq)])

    def core_permute(x):
        return lax.ppermute(x, "batch", [(b, b ^ 1) for b in range(n_batch)])

    def take(x, i):
        return lax.dynamic_index_in_dim(x, i, 0, keepdims=False)

    def two(flag, mine, theirs, axis):
        return jnp.where(flag == 0, jnp.stack([mine, theirs], axis), jnp.stack([theirs, mine], axis))

    def gather_plane(x, core, seq, *others):
        if n_seq != 4:
            whole = lax.all_gather(x, BOTH, axis_index_groups=plane_groups, axis=0, tiled=True)
            whole = whole.reshape((CORES, n_seq * x.shape[0]) + x.shape[1:])
            return take(whole, core), take(whole, 1 - core), whole
        bit_x, bit_y = seq % 2, seq // 2
        half = x.shape[1] // 2
        left, right = x[:, :half], x[:, half:]
        left = two(bit_y, left, seq_permute(left, 2), 0)
        right = two(bit_x, right, seq_permute(right, 1), 0)
        early = left
        left = after(left, *others)
        left = two(bit_x, left, seq_permute(left, 1), 1)
        right = two(bit_y, right, seq_permute(right, 2), 0)
        own = jnp.concatenate([left, right], axis=3).reshape(4 * x.shape[0], x.shape[1])
        return own, core_permute(own), early

    def scatter_plane(product, tokens, core, seq):
        if n_seq != 4:
            both = [product(core ^ i) for i in range(CORES)]
            x = lax.psum_scatter(
                jnp.concatenate(both), BOTH, axis_index_groups=plane_groups, scatter_dimension=0, tiled=True
            ).astype(f32)
            return x, (x, x, x)
        other = core_permute(product(jnp.int32(1)))
        x = product(jnp.int32(0)).astype(f32) + other.astype(f32)
        x = x.astype(bf16).reshape(2, 2, tokens // n_seq, x.shape[1])
        bit_x, bit_y = seq % 2, seq // 2
        half = x.shape[3] // 2
        left, right = x[..., :half], x[..., half:]
        by_x = jnp.swapaxes(left, 0, 1)
        from_x = seq_permute(take(by_x, 1 - bit_x), 1)
        from_y = seq_permute(take(right, 1 - bit_y), 2)
        left = (take(by_x, bit_x).astype(f32) + from_x.astype(f32)).astype(bf16)
        right = (take(right, bit_y).astype(f32) + from_y.astype(f32)).astype(bf16)
        from_y = seq_permute(take(left, 1 - bit_y), 2)
        from_x = seq_permute(take(right, 1 - bit_x), 1)
        stages = (x, left, right)
        left = take(left, bit_y).astype(f32) + from_y.astype(f32)
        right = take(right, bit_x).astype(f32) + from_x.astype(f32)
        return jnp.concatenate([left, right], axis=1), stages

    def swap_plane(x):
        return lax.all_to_all(x, BOTH, 0, 0, axis_index_groups=plane_groups, tiled=True)

    def gather_line(x):
        return lax.all_gather(x, "batch", axis_index_groups=line_groups, axis=0, tiled=True)

    def scatter_line(x):
        return lax.psum_scatter(
            x, "batch", axis_index_groups=line_groups, scatter_dimension=0, tiled=True
        )

    class Chain:
        def __init__(self, x, plane):
            self.x, self.plane, self.step = x, plane, 0
            self.up = self.down = None

        def hop(self, *others):
            self.step += 1
            left = planes - self.step
            up = take(self.x, jnp.minimum(left + self.plane, planes - 1))
            down = take(self.x, jnp.maximum(self.plane - left, 0))
            if self.step > 1:
                up = (up.astype(f32) + self.up.astype(f32)).astype(bf16)
                down = (down.astype(f32) + self.down.astype(f32)).astype(bf16)
            up, down = after(up, *others), after(down, *others)
            self.up = lax.ppermute(up, "batch", [(b, b + CORES) for b in range(CORES * self.step)])
            self.down = lax.ppermute(down, "batch", [(b, b - CORES) for b in range(CORES * left, n_batch)])
            return self.up, self.down

        def result(self):
            while self.step < planes - 1:
                self.hop()
            return take(self.x, self.plane).astype(f32) + self.up.astype(f32) + self.down.astype(f32)

    def shards(
        tokens, segments, positions, cotangent, ln_gain, ln_bias, in_weight, in_bias, proj_weight, down_weight, out_bias
    ):
        rows, width = tokens.shape[1:]
        length = rows * n_seq
        in_rows, total = in_weight.shape
        proj_rows, down_rows = proj_weight.shape[0], down_weight.shape[0]
        hidden = total - 3 * width
        chunks = 2
        part = down_rows // chunks
        whole_heads = proj_rows % HD == 0
        head_groups = planes if whole_heads else 1
        head_cols = width // (head_groups * ranks)
        mine_cols = width // ranks
        index = lax.axis_index("batch") * n_seq + lax.axis_index("seq")
        rank = index % ranks
        plane = index // ranks
        core, seq = rank // n_seq, rank % n_seq

        def split_heads(x):
            lead = x.shape[0]
            x = x.reshape(lead, 3, head_groups, ranks, head_cols)
            return jnp.transpose(x, (3, 0, 1, 2, 4)).reshape(ranks, lead, 3 * mine_cols)

        def split_hidden(x, c):
            lead = x.shape[0]
            x = x.reshape(lead, planes, ranks, chunks, part)[:, :, :, c]
            return jnp.transpose(x, (2, 0, 1, 3)).reshape(ranks, lead, planes * part)

        def join_heads(x):
            lead = x.shape[1]
            x = x.reshape(ranks, lead, 3, head_groups, head_cols)
            return jnp.transpose(x, (1, 2, 3, 0, 4)).reshape(lead, 3 * width)

        def join_hidden(xs):
            lead = xs[0].shape[1]
            x = jnp.stack([x.reshape(ranks, lead, planes, part) for x in xs])
            return jnp.transpose(x, (2, 3, 1, 0, 4)).reshape(lead, hidden)

        def swap_columns(x):
            return swap_plane(x).reshape(ranks * in_rows, x.shape[2])

        units = planes * part
        first_send = swap_columns(
            jnp.concatenate(
                [split_hidden(in_weight[:, 3 * width :], 0), split_heads(in_weight[:, : 3 * width])], axis=2
            )
        )
        token_halves = gather_plane(tokens[0], core, seq)
        grad_halves = gather_plane(after(cotangent[0], token_halves[2]), core, seq)
        small = jnp.concatenate([x.astype(f32) for x in (in_bias, ln_gain, ln_bias, out_bias, positions[0])])
        small_all = lax.all_to_all(
            jnp.broadcast_to(after(small, token_halves[2])[None], (n_dev, small.shape[0])), BOTH, 0, 0, tiled=True
        )
        n_bias = in_bias.shape[0]
        n_width = ln_gain.shape[0]
        bias_all = small_all[:, :n_bias].reshape(-1)
        gain_all = small_all[:, n_bias : n_bias + n_width].reshape(-1)
        shift_all = small_all[:, n_bias + n_width : n_bias + 2 * n_width].reshape(-1)
        out_bias_all = small_all[:, n_bias + 2 * n_width : n_bias + 3 * n_width].reshape(-1)
        place = small_all[:, n_bias + 3 * n_width :].reshape(planes, CORES, length)
        place = lax.dynamic_index_in_dim(place, plane, 0, keepdims=False).astype(jnp.int32)
        place = jnp.concatenate([take(place, core), take(place, 1 - core)])

        bias_heads = lax.dynamic_index_in_dim(
            split_heads(bias_all[None, : 3 * width]), rank, 0, keepdims=False
        )
        bias_hidden = [
            lax.dynamic_index_in_dim(split_hidden(bias_all[None, 3 * width :], c), rank, 0, keepdims=False)
            for c in range(chunks)
        ]

        def own_columns(x):
            return swap_plane(x.reshape(ranks, in_rows, x.shape[1]))

        own_parts = []
        def unpack(x, few):
            lead, packed, total = x.shape
            columns = few * width // packed
            extra = x[:, :, total - columns :].reshape(lead, width // columns, few, columns)
            return x[:, :, : total - columns], jnp.swapaxes(extra, 1, 2).reshape(lead, few, width)

        down, w_hidden = [None] * chunks, [None] * chunks
        activated, grad_u, sum_u, grad_down, grad_hidden = [], [], [], [], []

        def hidden_part(c, *others):
            act, du, total = hidden_layer(normed, after(grad_all, *others), w_hidden[c], down[c], bias_hidden[c][0])
            activated.append(act)
            grad_u.append(du)
            sum_u.append(total)
            return dot(normed, du, TN).astype(bf16), dot(act, grad_all, TN).astype(bf16)

        normed = over_both(norm_kernel, *token_halves[:2], gain_all, shift_all)
        grad_all = over_both(join_kernel, *grad_halves[:2])
        def gather_packed(main, c, *others):
            x = pack(main[None], down_weight[None, c * part : (c + 1) * part])[0]
            x = gather_line(after(x, *others))
            down[c] = unpack(x.reshape(planes, ranks * in_rows, -1), part)[1].reshape(-1, width)
            return x

        if whole_heads:
            proj = gather_line(proj_weight)
        else:
            proj = lax.dynamic_slice_in_dim(
                lax.all_gather(proj_weight, BOTH, axis=0, tiled=True), rank * mine_cols, mine_cols, 0
            )
        x = gather_packed(first_send, 0, proj)
        w_hidden[0], w_heads = x[:, :units], x[:, units : units + 3 * mine_cols]
        for c in range(1, chunks):
            more = split_hidden(in_weight[:, 3 * width :], c)
            w_hidden[c] = gather_packed(swap_columns(after(more, token_halves[0])), c, x, normed, grad_all)[:, :units]
        by_plane = (planes, width // planes, -1)

        def scatter_packed(main, extra, few):
            x = pack(main.reshape(by_plane), extra.reshape(planes, few, width))
            x, y = unpack(scatter_line(x.reshape(width, -1))[None], few)
            return x[0], y[0].astype(f32)

        to_hidden, to_down = hidden_part(0)
        first, second = scatter_packed(to_hidden, to_down, part)
        grad_hidden.append(own_columns(first))
        grad_down.append(second)
        mixed, grad_attended = heads_layer(normed, after(grad_all, to_hidden, to_down), w_heads, proj, bias_heads[0])
        cosine, sine = rotary_wide(place)
        start = (jnp.arange(place.shape[0], dtype=jnp.int32) % length - place)[:, None]
        attended, grad_mixed = attention(mixed, grad_attended, cosine, sine, start, length)
        to_proj = dot(attended, grad_all, TN).astype(bf16)
        to_heads = dot(normed, grad_mixed, TN).astype(bf16)
        if whole_heads:
            grad_heads, grad_proj = scatter_packed(to_heads, to_proj, proj_rows)
        else:
            grad_heads = scatter_line(to_heads)
            grad_proj = lax.psum_scatter(
                lax.dynamic_update_slice_in_dim(
                    jnp.zeros((width, width), f32), to_proj.astype(f32), rank * mine_cols, 0
                ),
                BOTH, scatter_dimension=0, tiled=True,
            )

        last = []
        for c in range(1, chunks):
            last += hidden_part(c, to_heads, to_proj)
        bias_heads_sum = jnp.sum(grad_mixed.astype(f32), axis=0)
        grad_mixed = after(grad_mixed, *last)
        grad_normed, stages = scatter_plane(
            lambda i: joined_product([grad_mixed] + grad_u, [w_heads] + w_hidden, NT, i, length), length, core, seq
        )
        attended = after(attended, *last, stages[0], grad_hidden[0])
        out, more = scatter_plane(
            lambda i: joined_product([attended] + activated, [proj] + down, NN, i, length), length, core, seq
        )
        grad_heads = after(grad_heads, more[0])
        for c in range(1, chunks):
            to_hidden, to_down = last[2 * c - 2 : 2 * c]
            grad_hidden.append(scatter_line(after(to_hidden, stages[0])))
            grad_down.append(scatter_line(after(to_down, *stages, grad_hidden[c])).astype(f32))

        own = tokens[0].astype(f32)
        own_grad = cotangent[0].astype(f32)
        result = own + out + out_bias_all
        centred = own - jnp.mean(own, axis=1, keepdims=True)
        inv_std = lax.rsqrt(jnp.mean(centred * centred, axis=1, keepdims=True) + NORM_EPS)
        normal = centred * inv_std
        scaled = grad_normed * gain_all
        grad_tokens = own_grad + inv_std * (
            scaled
            - jnp.mean(scaled, axis=1, keepdims=True)
            - normal * jnp.mean(scaled * normal, axis=1, keepdims=True)
        )

        last = [result, grad_tokens]
        grad_hidden[1:] = [after(x, *last) for x in grad_hidden[1:]]
        grad_down[1:] = [after(x, *last) for x in grad_down[1:]]

        def full_columns(heads_part, hidden_parts):
            at = (jnp.arange(ranks) == rank)[:, None, None]
            heads_all = join_heads(jnp.where(at, heads_part[None, None], 0.0))
            hidden_all = join_hidden([jnp.where(at, x[None, None], 0.0) for x in hidden_parts])
            return jnp.concatenate([heads_all, hidden_all], axis=1)

        bias_sum = full_columns(
            bias_heads_sum, [x[0] for x in sum_u]
        )
        sums = jnp.concatenate(
            [
                bias_sum.reshape(n_dev, n_bias),
                jnp.sum(grad_normed * normal, axis=0).reshape(n_dev, n_width),
                jnp.sum(grad_normed, axis=0).reshape(n_dev, n_width),
                jnp.sum(own_grad, axis=0).reshape(n_dev, n_width),
            ],
            axis=1,
        )
        sums = jnp.sum(lax.all_to_all(sums, BOTH, 0, 0, tiled=True), axis=0)

        grad_in = jnp.concatenate(
            [join_heads(own_columns(grad_heads)), join_hidden(grad_hidden[:1] + [own_columns(x) for x in grad_hidden[1:]])], axis=1
        ).astype(f32)
        return (
            result.astype(bf16)[None],
            grad_tokens.astype(bf16)[None],
            sums[n_bias : n_bias + n_width],
            sums[n_bias + n_width : n_bias + 2 * n_width],
            grad_in,
            sums[:n_bias],
            grad_proj,
            jnp.concatenate(grad_down, axis=0).astype(f32),
            sums[n_bias + 2 * n_width :],
        )

    return shards


def solution(mesh):
    placed = (
        P("batch", "seq", None),
        P("batch", "seq"),
        P("batch", "seq"),
        P("batch", "seq", None),
        P(("batch", "seq")),
        P(("batch", "seq")),
        P(("batch", "seq"), None),
        P(("batch", "seq")),
        P(("batch", "seq"), None),
        P(("batch", "seq"), None),
        P(("batch", "seq")),
    )
    return jax.shard_map(
        build(mesh.shape["batch"], mesh.shape["seq"]),
        mesh=mesh,
        in_specs=placed,
        out_specs=(
            P("batch", "seq", None),
            P("batch", "seq", None),
            P(("batch", "seq")),
            P(("batch", "seq")),
            P(("batch", "seq"), None),
            P(("batch", "seq")),
            P(("batch", "seq"), None),
            P(("batch", "seq"), None),
            P(("batch", "seq")),
        ),
        check_vma=False,
    )
```
